512 devices in a mesh: head: 8 (over x, core), ctx: 64 (over y, z).
Axes of the slice: x: 4, y: 4, z: 16, core: 2. Of those that a mesh axis runs over, the one named last changes fastest.
Arguments:
- queries: bfloat16 [65536, 4096], P('ctx', 'head'), may hold values from -24 to 24
- keys: bfloat16 [65536, 1024], P('ctx', 'head'), may hold values from -24 to 24
- values: bfloat16 [65536, 1024], P('ctx', 'head'), may hold values from -6 to 6
- vertical_ids: int32 [8, 8], P('head'), may hold values from 0 to 511, as said below
- slash_offsets: int32 [8, 2], P('head'), may hold values from 1 to 8, as said below
- keep_counts: int32 [8, 512], P('head', 'ctx'), may hold values from 1 to 8
Outputs:
- attended: bfloat16 [65536, 4096], P('ctx', 'head')
- column_scores: float32 [65536], P('ctx')
- vertical_scores: float32 [8, 8, 128], P('head')
The draws below stay inside these ranges and needn't reach their ends.
Inputs may be any that keep to these rules, and one draw needn't show every extreme that they name: `vertical_ids`: the entries of a row are distinct and the first is 0. `slash_offsets`: the entries of a row are distinct and the first is 8.
All inputs are finite; a program needn't handle non-finite values.
Results may differ from the reference program's by a relative error of at most 0.0049.
Values may be sent and summed in bfloat16 or wider, within the bound.
A program may use at most 64 MiB of HBM per device.

```python
import jax
import jax.numpy as jnp
from jax import lax

HD = 128
QPK = 4
KVH = 8
TILE = 128
NV = 8
NS = 2
TILES_DEV = 8
TOKENS = 65536
ALL_TILES = 512


def draw_keys(key, part):
    key = jax.random.fold_in(key, 11)
    drawn = jnp.clip(jax.random.normal(key, (TOKENS, KVH, HD), jnp.float32), -4.0, 4.0)
    return drawn.reshape(TOKENS, KVH * HD).astype(jnp.bfloat16)


def draw_queries(key, part):
    key = jax.random.fold_in(key, 12)
    drawn = jnp.clip(jax.random.normal(key, (TOKENS, KVH, QPK, HD), jnp.float32), -4.0, 4.0)
    return drawn.reshape(TOKENS, KVH * QPK * HD).astype(jnp.bfloat16)


def draw_vertical_ids(key, part):
    key = jax.random.fold_in(key, 21)
    head_keys = jax.random.split(key, KVH)
    picks = jax.vmap(lambda one_key: jax.random.permutation(one_key, ALL_TILES - 1)[:NV - 1] + 1)(head_keys)
    return jnp.concatenate([jnp.zeros((KVH, 1), jnp.int32), picks.astype(jnp.int32)], axis=1)


def draw_slash_offsets(key, part):
    key = jax.random.fold_in(key, 22)
    head_keys = jax.random.split(key, KVH)
    picks = jax.vmap(lambda one_key: jax.random.permutation(one_key, TILES_DEV - 1)[:NS - 1] + 1)(head_keys)
    return jnp.concatenate([jnp.full((KVH, 1), TILES_DEV, jnp.int32), picks.astype(jnp.int32)], axis=1)


def draw_keep_counts(key, part):
    key = jax.random.fold_in(key, 23)
    counts = jax.random.randint(key, (KVH, ALL_TILES), 1, NV + 1).astype(jnp.int32)
    return counts.at[:, ALL_TILES - 1].set(NV)


def levels(own_key, extent, pieces, smallest, top_value):
    level = 1.0
    for position, blocks in pieces:
        steps = jax.random.uniform(jax.random.fold_in(jax.random.fold_in(own_key, 6), position), (blocks,), jnp.float32, smallest / len(pieces), top_value / len(pieces))
        level = level * jnp.repeat(jnp.exp(steps), extent[position] // blocks).reshape((-1,) + (1,) * (len(extent) - 1 - position))
    return level


def gaussian(rng, extent, spread, reach, pieces=(), kind=jnp.bfloat16):
    values = spread * jax.random.normal(rng, extent, jnp.float32)
    if pieces:
        values = values * levels(rng, extent, pieces, -0.22, 0.18)
    return jnp.clip(values, -reach, reach).astype(kind)


def setup_inputs(seed: int = 0) -> dict:
    arg_keys = jax.random.split(jax.random.key(seed), 7)
    return {
        "queries": draw_queries(jax.random.fold_in(arg_keys[6], 71), 0),
        "keys": draw_keys(jax.random.fold_in(arg_keys[6], 71), 0),
        "values": gaussian(arg_keys[2], (TOKENS, KVH * HD), 1.0, 6.0, ((0, 64), (1, 8))),
        "vertical_ids": draw_vertical_ids(jax.random.fold_in(arg_keys[6], 71), 0),
        "slash_offsets": draw_slash_offsets(jax.random.fold_in(arg_keys[6], 71), 0),
        "keep_counts": draw_keep_counts(jax.random.fold_in(arg_keys[6], 71), 0),
    }


def tile_attention(query_tile, key_rows, value_rows, valid, causal):
    scores = jnp.einsum("iqd,ckd->qick", query_tile.astype(jnp.float32), key_rows.astype(jnp.float32)) * (HD ** -0.5)
    mask = valid[None, None, :, None] & causal[None, :, :, :]
    scores = jnp.where(mask, scores, -1e30)
    row_max = jnp.max(scores, axis=(2, 3), keepdims=True)
    unnormed = jnp.exp(scores - row_max)
    totals = jnp.sum(unnormed, axis=(2, 3), keepdims=True)
    probs = unnormed / totals
    rounded = lax.optimization_barrier(probs.astype(jnp.bfloat16))
    mixed = jnp.einsum("qick,ckd->iqd", rounded.astype(jnp.float32), value_rows.astype(jnp.float32))
    return mixed.astype(jnp.bfloat16), jnp.sum(probs, axis=(0, 1))


def reference(queries, keys, values, vertical_ids, slash_offsets, keep_counts):
    query_tiles = queries.reshape(ALL_TILES, TILE, KVH, QPK, HD)
    key_tiles = keys.reshape(ALL_TILES, TILE, KVH, HD)
    value_tiles = values.reshape(ALL_TILES, TILE, KVH, HD)
    positions = jnp.arange(TILE, dtype=jnp.int32)
    slot_numbers = jnp.arange(1 + NS + NV, dtype=jnp.int32)
    causal = (slot_numbers[None, :, None] != 0) | (positions[None, None, :] <= positions[:, None, None])

    def group_tile(tile_index, group):
        slash_ids = (tile_index - slash_offsets[group]).astype(jnp.int32)
        slash_valid = slash_ids >= 0
        vertical = vertical_ids[group]
        repeated = jnp.any((vertical[:, None] == slash_ids[None, :]) & slash_valid[None, :], axis=1) | (vertical == tile_index)
        vertical_valid = (jnp.arange(NV, dtype=jnp.int32) < keep_counts[group, tile_index]) & (vertical <= tile_index) & jnp.logical_not(repeated)
        candidates = jnp.concatenate([tile_index[None].astype(jnp.int32), slash_ids, vertical.astype(jnp.int32)])
        valid = jnp.concatenate([jnp.ones((1,), bool), slash_valid, vertical_valid])
        safe_ids = jnp.clip(candidates, 0, ALL_TILES - 1).astype(jnp.int32)
        chosen_keys = key_tiles[safe_ids, :, group]
        chosen_values = value_tiles[safe_ids, :, group]
        query_tile = query_tiles[tile_index, :, group]
        mixed, columns = tile_attention(query_tile, chosen_keys, chosen_values, valid, causal)
        return mixed, columns, safe_ids

    def step(carry, tile_index):
        window_carry, vertical_carry = carry
        mixed, columns, safe_ids = jax.vmap(group_tile, in_axes=(None, 0))(tile_index, jnp.arange(KVH, dtype=jnp.int32))
        window_carry = window_carry.at[safe_ids[:, : 1 + NS].reshape(-1)].add(columns[:, : 1 + NS].reshape(-1, TILE))
        vertical_carry = vertical_carry + columns[:, 1 + NS:]
        return (window_carry, vertical_carry), jnp.transpose(mixed, (1, 0, 2, 3)).reshape(TILE, KVH * QPK * HD)

    start = (jnp.zeros((ALL_TILES, TILE), jnp.float32), jnp.zeros((KVH, NV, TILE), jnp.float32))
    (window_columns, vertical_columns), outputs = lax.scan(step, start, jnp.arange(ALL_TILES, dtype=jnp.int32))
    return outputs.reshape(TOKENS, KVH * QPK * HD), window_columns.reshape(TOKENS) / (KVH * QPK), vertical_columns / QPK
```

```python
import functools
import math

import jax
import jax.numpy as jnp
from jax import lax
from jax.experimental import pallas as pl
from jax.experimental.pallas import tpu as pltpu
from jax.sharding import PartitionSpec as P

MESH = pl.DeviceIdType.MESH
QPK = 4
TILE = 128
HD = 128
NV = 8
NT = 8
ROWS = QPK * TILE
NG = 2
G = NV // NG
NY = 4
NL = 4
NH = 4
HEADS = 8
CTX = NY * NL * NH
HIDE = -1e30
RATE = HD ** -0.5 * math.log2(math.e)
F32 = jnp.float32
BF16 = jnp.bfloat16


def dot_nt(a, b):
    return lax.dot_general(a, b, (((1,), (1,)), ((), ())), preferred_element_type=F32)


def kernel(vert, slash, keep, q_hbm, k_hbm, v_hbm, att_hbm, col_ref, ver_ref,
           q, ko, vo, kw, vw, kvert, vvert, att, causal, ebuf_a, ebuf_b, mx, acc, win, vs,
           s1, r1a, r1b, s2, r2a, r2b, s3, r3a, r3b, full,
           hs, hr, rw, v1, v2, v3,
           in_sem, out_sem, slash_s, slash_r, ex_s, ex_r, t_s, t_r, h_s, h_r):
    head = lax.axis_index("head")
    ctx = lax.axis_index("ctx")
    y = ctx // (NL * NH)
    zh = (ctx // NL) % NH
    zl = ctx % NL

    def at(a, b, c):
        return (head, a * (NL * NH) + b * NL + c)

    y_peers = [((y + k) % NY, at((y + k) % NY, zh, zl)) for k in (1, 2, 3)]
    l_peers = [((zl + k) % NL, at(y, zh, (zl + k) % NL)) for k in (1, 2, 3)]
    h_peers = [((zh + k) % NH, at(y, (zh + k) % NH, zl)) for k in (1, 2, 3)]
    heads = [((head + k) % HEADS, ((head + k) % HEADS, ctx)) for k in range(1, HEADS)]
    after = (head, (ctx + 1) % CTX)
    before = (head, (ctx + CTX - 1) % CTX)

    barrier = pltpu.get_barrier_semaphore()
    greeted = [p for _, p in y_peers + l_peers + h_peers + heads] + [after, before]
    for p in greeted:
        pl.semaphore_signal(barrier, inc=1, device_id=p, device_id_type=MESH)

    loads = [
        pltpu.make_async_copy(k_hbm, ko, in_sem.at[0]),
        pltpu.make_async_copy(v_hbm, vo, in_sem.at[1]),
        pltpu.make_async_copy(q_hbm, q, in_sem.at[2]),
        pltpu.make_async_copy(k_hbm, kw.at[pl.ds(NT, NT)], in_sem.at[3]),
        pltpu.make_async_copy(v_hbm, vw.at[pl.ds(NT, NT)], in_sem.at[4]),
    ]
    for c in loads:
        c.start()

    def remote(src, dst, ss, rs, p):
        return pltpu.make_async_remote_copy(
            src_ref=src, dst_ref=dst, send_sem=ss, recv_sem=rs, device_id=p, device_id_type=MESH
        )

    row = lax.broadcasted_iota(jnp.int32, (ROWS, HD), 0) % TILE
    lane = lax.broadcasted_iota(jnp.int32, (ROWS, HD), 1)
    causal[...] = jnp.where((lane == 0) | (lane > row), 1.0, 0.0).astype(BF16)
    win[...] = jnp.zeros_like(win)
    vs[...] = jnp.zeros_like(vs)

    loads[0].wait()
    loads[1].wait()
    for j in range(NV):
        g, jj = divmod(j, G)
        for part, ref in ((0, ko), (1, vo)):
            tile = ref[vert[0, j] & (NT - 1)]
            for half in range(2):
                s1[g, 2 * part + half, jj] = tile[64 * half:64 * half + 64]
    r1 = (r1a, r1b)
    r2 = (r2a, r2b)
    r3 = (r3a, r3b)
    for g in range(NG):
        r1[g][y] = s1[g, y]

    pl.semaphore_wait(barrier, len(greeted))

    def stage(g, number, peers, src, dst):
        base = (g * 5 + number) * 3
        return [
            remote(src(i), dst(i), ex_s.at[base + n], ex_r.at[base + n], p)
            for n, (i, p) in enumerate(peers)
        ]

    steps = {}
    for g in range(NG):
        steps[g, 0] = stage(g, 0, y_peers, lambda i: s1.at[g, i], lambda i: r1[g].at[y])
        for c in steps[g, 0]:
            c.start()
    slash_copies = [
        remote(ko, kw.at[pl.ds(0, NT)], slash_s.at[0], slash_r.at[0], after),
        remote(vo, vw.at[pl.ds(0, NT)], slash_s.at[1], slash_r.at[1], after),
    ]
    for c in slash_copies:
        c.start()

    def owner(j, low, count):
        return (vert[0, j] >> low) & (count - 1)

    def arrived(g, number):
        for c in steps[g, number]:
            c.wait_recv()

    for g in range(NG):
        arrived(g, 0)
        for jj in range(G):
            src = owner(g * G + jj, 7, NY)
            block = r1[g][src, jj]
            for r in range(NL):
                s2[g, r, jj] = block[16 * r:16 * r + 16]
        r2[g][zl] = s2[g, zl]
        steps[g, 1] = stage(g, 1, l_peers, lambda i: s2.at[g, i], lambda i: r2[g].at[zl])
        for c in steps[g, 1]:
            c.start()
    for g in range(NG):
        arrived(g, 1)
        for jj in range(G):
            s3[g, jj] = r2[g][owner(g * G + jj, 3, NL), jj]
        r3[g][zh] = s3[g]
        steps[g, 2] = stage(g, 2, h_peers, lambda i: s3.at[g], lambda i: r3[g].at[zh])
        for c in steps[g, 2]:
            c.start()

    for c in loads[2:]:
        c.wait()
    for c in slash_copies:
        c.wait_recv()
    key_row = lax.broadcasted_iota(jnp.int32, (TILE, HD), 0)
    key_lane = lax.broadcasted_iota(jnp.int32, (TILE, HD), 1)
    near = slash[0, 1]

    def stacked(i):
        rows = q[pl.ds(pl.multiple_of(i * TILE, TILE), TILE), :]
        return jnp.concatenate([rows[:, h * HD:(h + 1) * HD] for h in range(QPK)], axis=0)

    def soft(scores):
        top = jnp.max(scores, axis=1, keepdims=True)
        return top, jnp.exp2((scores - top) * RATE).astype(BF16)

    def mixed(weights, value_rows):
        ones = jnp.ones(value_rows.shape, BF16)
        return jnp.dot(weights, jnp.concatenate([value_rows, ones], axis=1), preferred_element_type=F32)

    def first(i, _):
        t = ctx * NT + i
        keys = jnp.concatenate([kw[NT + i], kw[i], kw[NT + i - near]], axis=0)
        values = jnp.concatenate([vw[NT + i], vw[i], vw[NT + i - near]], axis=0)
        diagonal = jnp.where((key_row == key_lane) & (key_lane > 0), HIDE, 0.0).astype(BF16)
        far_bias = jnp.where((key_lane == 0) & (key_lane + t < slash[0, 0]), HIDE, 0.0).astype(BF16)
        near_bias = jnp.where((key_lane == 0) & (key_lane + t < near), HIDE, 0.0).astype(BF16)
        bias = jnp.concatenate([diagonal, far_bias, near_bias], axis=0)
        query = jnp.concatenate([stacked(i), causal[...]], axis=1)
        scores = dot_nt(query, jnp.concatenate([keys, bias], axis=1))
        top, weights = soft(scores)
        ebuf_a[i] = weights
        mx[0, i] = jnp.broadcast_to(top, (ROWS, HD))
        acc[i] = mixed(weights, values)
        return 0

    lax.fori_loop(0, NT, first, 0)

    for g in range(NG):
        arrived(g, 2)
        for jj in range(G):
            full[g, 4 * y + zl, jj] = r3[g][owner(g * G + jj, 5, NH), jj]
        steps[g, 3] = stage(g, 3, l_peers, lambda i: full.at[g, 4 * y + zl], lambda i: full.at[g, 4 * y + zl])
        for c in steps[g, 3]:
            c.start()
    for g in range(NG):
        arrived(g, 3)
        mine = pl.ds(4 * y, 4)
        steps[g, 4] = stage(g, 4, y_peers, lambda i: full.at[g, mine], lambda i: full.at[g, mine])
        for c in steps[g, 4]:
            c.start()

    lanes8 = lax.broadcasted_iota(jnp.int32, (8, HD), 1)
    ids = jnp.zeros((8, HD), jnp.int32)
    for j in range(NV):
        ids = jnp.where(lanes8 == j, vert[0, j], ids)
    slot_row = lax.broadcasted_iota(jnp.int32, (G * TILE, HD), 0) // TILE
    slot_lane = lax.broadcasted_iota(jnp.int32, (G * TILE, HD), 1)

    def flags(i):
        t = ctx * NT + i
        valid = (lanes8 < keep[0, i]) & (ids < t) & (ids != t - slash[0, 0]) & (ids != t - near)
        flag = jnp.where(valid | (lanes8 >= NV), 0.0, 1.0)
        return jnp.broadcast_to(flag[:1], (ROWS, HD)).astype(BF16)

    for g in range(NG):
        arrived(g, 4)
        for jj in range(G):
            kvert[g, jj] = jnp.concatenate([full[g, p, jj] for p in range(8)], axis=0)
            vvert[g, jj] = jnp.concatenate([full[g, 8 + p, jj] for p in range(8)], axis=0)
        bias = jnp.where(slot_row + g * G == slot_lane, HIDE, 0.0).astype(BF16)

        def vertical(i, _):
            keys = kvert[g].reshape(G * TILE, HD)
            values = vvert[g].reshape(G * TILE, HD)
            query = jnp.concatenate([stacked(i), flags(i)], axis=1)
            scores = dot_nt(query, jnp.concatenate([keys, bias], axis=1))
            top, weights = soft(scores)
            ebuf_b[g, i] = weights
            new = jnp.broadcast_to(top, (ROWS, HD))
            old = mx[g, i]
            top = jnp.maximum(old, new)
            mx[g + 1, i] = top
            before_scale = jnp.exp2((old - top) * RATE)
            now_scale = jnp.exp2((new - top) * RATE)
            part = mixed(weights, values)
            held = acc[i]
            acc[i] = jnp.concatenate(
                [held[:, :HD] * before_scale + part[:, :HD] * now_scale,
                 held[:, HD:] * before_scale + part[:, HD:] * now_scale], axis=1)
            hs[g, i] = new
            return 0

        lax.fori_loop(0, NT, vertical, 0)

    lane_id = lax.broadcasted_iota(jnp.int32, (ROWS, HD), 1)
    win_row = lax.broadcasted_iota(jnp.int32, (2 * NT, TILE), 0)
    vs_row = lax.broadcasted_iota(jnp.int32, (NV, TILE), 0)

    def finish(i, _):
        held = acc[i]
        inverse = 1.0 / held[:, HD:]
        out = (held[:, :HD] * inverse).astype(BF16)
        here = pl.ds(pl.multiple_of(i * TILE, TILE), TILE)
        att[here, :] = jnp.concatenate([out[h * TILE:(h + 1) * TILE] for h in range(QPK)], axis=1)
        pltpu.make_async_copy(att.at[here, :], att_hbm.at[here, :], out_sem.at[i]).start()
        top = mx[NG, i]
        factors = jnp.exp2((mx[0, i] - top) * RATE) * inverse
        for g in range(NG):
            factors = jnp.where(lane_id == g + 1, jnp.exp2((hs[g, i] - top) * RATE) * inverse, factors)
        turned = jnp.transpose(factors)[:8]
        high = turned.astype(BF16)
        low = (turned - high.astype(F32)).astype(BF16)
        rows = jnp.concatenate([high, low], axis=0)

        def sums(weights, which):
            both = jnp.dot(rows, weights, preferred_element_type=F32)
            return both[which:which + 1] + both[8 + which:9 + which]

        near_sums = sums(ebuf_a[i], 0)
        add = jnp.where(win_row == NT + i, near_sums[:, :TILE], 0.0)
        add = add + jnp.where(win_row == i, near_sums[:, TILE:2 * TILE], 0.0)
        add = add + jnp.where(win_row == NT + i - near, near_sums[:, 2 * TILE:], 0.0)
        win[...] += add
        total = vs[...]
        for g in range(NG):
            part = sums(ebuf_b[g, i], g + 1)
            for jj in range(G):
                total = total + jnp.where(vs_row == g * G + jj, part[:, jj * TILE:(jj + 1) * TILE], 0.0)
        vs[...] = total
        return 0

    lax.fori_loop(0, NT, finish, 0)

    to_before = remote(win.at[pl.ds(0, NT)], rw, h_s.at[7], h_r.at[7], before)
    to_before.start()
    v1[y] = vs[...]
    c1 = [remote(vs, v1.at[y], t_s.at[n], t_r.at[n], p) for n, (_, p) in enumerate(y_peers)]
    for c in c1:
        c.start()
    to_before.wait_recv()
    hr[head] = win[NT:] + rw[...]
    ch = [remote(hr.at[head], hr.at[head], h_s.at[n], h_r.at[n], p) for n, (_, p) in enumerate(heads)]
    for c in ch:
        c.start()
    for c in c1:
        c.wait_recv()
    v2[zl] = (v1[0] + v1[1]) + (v1[2] + v1[3])
    c2 = [remote(v2.at[zl], v2.at[zl], t_s.at[3 + n], t_r.at[3 + n], p) for n, (_, p) in enumerate(l_peers)]
    for c in c2:
        c.start()
    for c in c2:
        c.wait_recv()
    v3[zh] = (v2[0] + v2[1]) + (v2[2] + v2[3])
    c3 = [remote(v3.at[zh], v3.at[zh], t_s.at[6 + n], t_r.at[6 + n], p) for n, (_, p) in enumerate(h_peers)]
    for c in c3:
        c.start()
    for c in ch:
        c.wait_recv()
    total = hr[0]
    for n in range(1, HEADS):
        total = total + hr[n]
    col_ref[...] = total * (1.0 / (HEADS * QPK))
    for c in c3:
        c.wait_recv()
    ver_ref[0] = ((v3[0] + v3[1]) + (v3[2] + v3[3])) * (1.0 / QPK)

    for c in [c for group in steps.values() for c in group] + slash_copies + [to_before] + c1 + c2 + c3 + ch:
        c.wait_send()
    for i in range(NT):
        here = pl.ds(i * TILE, TILE)
        pltpu.make_async_copy(att.at[here, :], att_hbm.at[here, :], out_sem.at[i]).wait()


def local(queries, keys, values, vertical_ids, slash_offsets, keep_counts):
    rows = keys.shape[0]
    smem = pl.BlockSpec(memory_space=pltpu.SMEM)
    vmem = pl.BlockSpec(memory_space=pltpu.VMEM)
    hbm = pl.BlockSpec(memory_space=pl.ANY)
    dma = pltpu.SemaphoreType.DMA
    attended, column, vertical = pl.pallas_call(
        kernel,
        out_shape=(
            jax.ShapeDtypeStruct(queries.shape, BF16),
            jax.ShapeDtypeStruct((NT, TILE), F32),
            jax.ShapeDtypeStruct((1, NV, TILE), F32),
        ),
        in_specs=[smem, smem, smem, hbm, hbm, hbm],
        out_specs=(hbm, vmem, vmem),
        scratch_shapes=[
            pltpu.VMEM((rows, QPK * HD), BF16),
            *[pltpu.VMEM((NT, TILE, HD), BF16) for _ in range(2)],
            *[pltpu.VMEM((2 * NT, TILE, HD), BF16) for _ in range(2)],
            *[pltpu.VMEM((NG, G, TILE, HD), BF16) for _ in range(2)],
            pltpu.VMEM((rows, QPK * HD), BF16),
            pltpu.VMEM((ROWS, HD), BF16),
            pltpu.VMEM((NT, ROWS, 3 * TILE), BF16),
            pltpu.VMEM((NG, NT, ROWS, G * TILE), BF16),
            pltpu.VMEM((NG + 1, NT, ROWS, HD), F32),
            pltpu.VMEM((NT, ROWS, 2 * HD), F32),
            pltpu.VMEM((2 * NT, TILE), F32),
            pltpu.VMEM((NV, TILE), F32),
            pltpu.VMEM((NG, NY, G, 64, HD), BF16),
            *[pltpu.VMEM((NY, G, 64, HD), BF16) for _ in range(2)],
            pltpu.VMEM((NG, NL, G, 16, HD), BF16),
            *[pltpu.VMEM((NL, G, 16, HD), BF16) for _ in range(2)],
            pltpu.VMEM((NG, G, 16, HD), BF16),
            *[pltpu.VMEM((NH, G, 16, HD), BF16) for _ in range(2)],
            pltpu.VMEM((NG, 16, G, 16, HD), BF16),
            pltpu.VMEM((NG, NT, ROWS, HD), F32),
            pltpu.VMEM((HEADS, NT, TILE), F32),
            pltpu.VMEM((NT, TILE), F32),
            pltpu.VMEM((NY, NV, TILE), F32),
            pltpu.VMEM((NL, NV, TILE), F32),
            pltpu.VMEM((NH, NV, TILE), F32),
            dma((5,)), dma((NT,)), dma((2,)), dma((2,)),
            dma((NG * 15,)), dma((NG * 15,)), dma((9,)), dma((9,)), dma((8,)), dma((8,)),
        ],
        compiler_params=pltpu.CompilerParams(
            collective_id=0, has_side_effects=True, vmem_limit_bytes=56 << 20
        ),
    )(vertical_ids, slash_offsets, keep_counts, queries, keys.reshape(NT, TILE, HD), values.reshape(NT, TILE, HD))
    return attended, column.reshape(rows), vertical


def solution(mesh):
    placed = (
        P("ctx", "head"),
        P("ctx", "head"),
        P("ctx", "head"),
        P("head", None),
        P("head", None),
        P("head", "ctx"),
    )
    return jax.shard_map(
        local,
        mesh=mesh,
        in_specs=placed,
        out_specs=(P("ctx", "head"), P("ctx"), P("head", None, None)),
        check_vma=False,
    )
```

```python
import functools
import math

import jax
import jax.numpy as jnp
from jax import lax
from jax.experimental import pallas as pl
from jax.experimental.pallas import tpu as pltpu
from jax.sharding import PartitionSpec as P

MESH = pl.DeviceIdType.MESH
QPK = 4
TILE = 128
HD = 128
NV = 8
NT = 8
ROWS = QPK * TILE
NG = 2
G = NV // NG
NY = 4
NL = 4
NH = 4
HEADS = 8
CTX = NY * NL * NH
HIDE = -1e30
RATE = HD ** -0.5 * math.log2(math.e)
NEAR = (-1, -2, 1)
SLASH_K = 0
SLASH_V = 2
F32 = jnp.float32
BF16 = jnp.bfloat16


def dot_nt(a, b):
    return lax.dot_general(a, b, (((1,), (1,)), ((), ())), preferred_element_type=F32)


def kernel(vert, slash, keep, q_hbm, k_hbm, v_hbm, att, col_ref, ver_ref,
           q, ko, vo, kw, vw, kvert, vvert, causal, ebuf_a, ebuf_b, mx, acc, win, vs,
           s1, r1a, r1b, s2, r2a, r2b, s3, r3a, r3b, full,
           hr, rw, v1, v2, v3,
           in_sem, slash_s, slash_r, ex_s, ex_r, last_s, last_r, t_s, t_r, h_s, h_r):
    head = lax.axis_index("head")
    ctx = lax.axis_index("ctx")
    y = ctx // (NL * NH)
    zh = (ctx // NL) % NH
    zl = ctx % NL
    z = ctx % (NL * NH)

    def at(a, b, c):
        return (head, a * (NL * NH) + b * NL + c)

    def along(k):
        return (head, y * (NL * NH) + (z + k + NL * NH) % (NL * NH))

    y_peers = [((y + k) % NY, at((y + k) % NY, zh, zl)) for k in (1, 2, 3)]
    l_peers = [((zl + k) % NL, at(y, zh, (zl + k) % NL)) for k in (1, 2, 3)]
    h_peers = [((zh + k) % NH, at(y, (zh + k) % NH, zl)) for k in (1, 2, 3)]
    n_peers = [((zl + k + NL) % NL, along(k)) for k in NEAR]
    heads = [((head + k) % HEADS, ((head + k) % HEADS, ctx)) for k in range(1, HEADS)]
    after = (head, (ctx + 1) % CTX)
    before = (head, (ctx + CTX - 1) % CTX)

    barrier = pltpu.get_barrier_semaphore()
    greeted = [p for _, p in h_peers + y_peers + l_peers + heads] + [after, before]
    greeted += [along(k) for k in (-2, -1, 1, 2)]
    for p in greeted:
        pl.semaphore_signal(barrier, inc=1, device_id=p, device_id_type=MESH)

    loads = [
        pltpu.make_async_copy(k_hbm, ko, in_sem.at[0]),
        pltpu.make_async_copy(v_hbm, vo, in_sem.at[1]),
        pltpu.make_async_copy(q_hbm, q, in_sem.at[2]),
        pltpu.make_async_copy(k_hbm, kw.at[pl.ds(NT, NT)], in_sem.at[3]),
        pltpu.make_async_copy(v_hbm, vw.at[pl.ds(NT, NT)], in_sem.at[4]),
    ]
    for c in loads:
        c.start()

    def remote(src, dst, ss, rs, p):
        return pltpu.make_async_remote_copy(
            src_ref=src, dst_ref=dst, send_sem=ss, recv_sem=rs, device_id=p, device_id_type=MESH
        )

    row = lax.broadcasted_iota(jnp.int32, (ROWS, HD), 0) % TILE
    lane = lax.broadcasted_iota(jnp.int32, (ROWS, HD), 1)
    causal[...] = jnp.where((lane == 0) | (lane > row), 1.0, 0.0).astype(BF16)
    win[...] = jnp.zeros_like(win)
    vs[...] = jnp.zeros_like(vs)

    loads[0].wait()
    loads[1].wait()
    for j in range(NV):
        g, jj = divmod(j, G)
        for part, ref in ((0, ko), (1, vo)):
            tile = ref[vert[0, j] & (NT - 1)]
            for piece in range(8):
                of_y, of_l = divmod(8 * part + piece, NL)
                rows = tile[16 * piece:16 * piece + 16]
                if g == 0:
                    s1[g, of_y, jj, 16 * of_l:16 * of_l + 16] = rows
                else:
                    s1[g, of_l, jj, 16 * of_y:16 * of_y + 16] = rows
    r1 = (r1a, r1b)
    r2 = (r2a, r2b)
    r3 = (r3a, r3b)
    mine = ((y, zl), (zl, y))
    peers = ((y_peers, n_peers), (n_peers, y_peers))
    for g in range(NG):
        r1[g][mine[g][0]] = s1[g, mine[g][0]]

    pl.semaphore_wait(barrier, len(greeted))

    def stage(g, number, peers, src, dst):
        base = (g * 5 + number) * 3
        return [
            remote(src(i), dst(i), ex_s.at[base + n], ex_r.at[base + n], p)
            for n, (i, p) in enumerate(peers)
        ]

    steps = {}
    for g in range(NG):
        steps[g, 0] = stage(g, 0, peers[g][0], lambda i: s1.at[g, i], lambda i: r1[g].at[mine[g][0]])
        for c in steps[g, 0]:
            c.start()
    lower = pl.ds(0, NT)
    slash_copies = [
        remote(ko, kw.at[lower], slash_s.at[0], slash_r.at[0], after),
        remote(vo, vw.at[lower], slash_s.at[1], slash_r.at[1], after),
    ]

    def send_slash(number):
        for c, when in zip(slash_copies, (SLASH_K, SLASH_V)):
            if when == number:
                c.start()

    send_slash(0)

    def owner(j, low, count):
        return (vert[0, j] >> low) & (count - 1)

    def arrived(g, number):
        for c in steps[g, number]:
            c.wait_recv()

    for g in range(NG):
        arrived(g, 0)
        for jj in range(G):
            j = g * G + jj
            src = owner(j, 7, NY) if g == 0 else owner(j, 3, NL)
            block = r1[g][src, jj]
            for n in range(4):
                s2[g, n, jj] = block[16 * n:16 * n + 16]
        r2[g][mine[g][1]] = s2[g, mine[g][1]]
        steps[g, 1] = stage(g, 1, peers[g][1], lambda i: s2.at[g, i], lambda i: r2[g].at[mine[g][1]])
        for c in steps[g, 1]:
            c.start()
    send_slash(1)
    for g in range(NG):
        arrived(g, 1)
        for jj in range(G):
            j = g * G + jj
            src = owner(j, 3, NL) if g == 0 else owner(j, 7, NY)
            s3[g, jj] = r2[g][src, jj]
        r3[g][zh] = s3[g]
        steps[g, 2] = stage(g, 2, h_peers, lambda i: s3.at[g], lambda i: r3[g].at[zh])
        for c in steps[g, 2]:
            c.start()
    send_slash(2)

    for c in loads[2:]:
        c.wait()
    slash_copies[0].wait_recv()
    key_row = lax.broadcasted_iota(jnp.int32, (TILE, HD), 0)
    key_lane = lax.broadcasted_iota(jnp.int32, (TILE, HD), 1)
    near = slash[0, 1]

    def stacked(i):
        rows = q[pl.ds(pl.multiple_of(i * TILE, TILE), TILE), :]
        return jnp.concatenate([rows[:, h * HD:(h + 1) * HD] for h in range(QPK)], axis=0)

    def soft(scores):
        top = jnp.max(scores, axis=1, keepdims=True)
        return top, jnp.exp2((scores - top) * RATE).astype(BF16)

    def mixed(weights, value_rows):
        ones = jnp.ones(value_rows.shape, BF16)
        return jnp.dot(weights, jnp.concatenate([value_rows, ones], axis=1), preferred_element_type=F32)

    def first(i, _):
        t = ctx * NT + i
        keys = jnp.concatenate([kw[NT + i], kw[i], kw[NT + i - near]], axis=0)
        diagonal = jnp.where((key_row == key_lane) & (key_lane > 0), HIDE, 0.0).astype(BF16)
        far_bias = jnp.where((key_lane == 0) & (key_lane + t < slash[0, 0]), HIDE, 0.0).astype(BF16)
        near_bias = jnp.where((key_lane == 0) & (key_lane + t < near), HIDE, 0.0).astype(BF16)
        bias = jnp.concatenate([diagonal, far_bias, near_bias], axis=0)
        query = jnp.concatenate([stacked(i), causal[...]], axis=1)
        scores = dot_nt(query, jnp.concatenate([keys, bias], axis=1))
        top, weights = soft(scores)
        ebuf_a[i] = weights
        mx[0, i] = jnp.broadcast_to(top, (ROWS, HD))
        return 0

    lax.fori_loop(0, NT, first, 0, unroll=4)

    piece = 4 * y + zl
    for g in range(NG):
        arrived(g, 2)
        for jj in range(G):
            j = g * G + jj
            of = owner(j, 3, NL * NH)
            gathered = (of + ((zl - of + 2) & (NL - 1)) - 2) & (NL * NH - 1)
            full[g, piece, jj] = r3[g][gathered >> 2, jj]
        steps[g, 3] = stage(g, 3, peers[g][1], lambda i: full.at[g, piece], lambda i: full.at[g, piece])
        for c in steps[g, 3]:
            c.start()
    send_slash(3)
    for g in range(NG):
        arrived(g, 3)
        if g == 0:
            block = pl.ds(4 * y, 4)
            steps[g, 4] = stage(g, 4, y_peers, lambda i: full.at[g, block], lambda i: full.at[g, block])
        else:
            steps[g, 4] = [
                remote(full.at[g, 4 * n + zl], full.at[g, 4 * n + zl], last_s.at[3 * n + k], last_r.at[3 * n + k], p)
                for n in range(NY)
                for k, (_, p) in enumerate(n_peers)
            ]
        for c in steps[g, 4]:
            c.start()
    send_slash(4)

    lanes8 = lax.broadcasted_iota(jnp.int32, (8, HD), 1)
    ids = jnp.zeros((8, HD), jnp.int32)
    for j in range(NV):
        ids = jnp.where(lanes8 == j, vert[0, j], ids)
    slot_row = lax.broadcasted_iota(jnp.int32, (G * TILE, HD), 0) // TILE
    slot_lane = lax.broadcasted_iota(jnp.int32, (G * TILE, HD), 1)

    def flags(i):
        t = ctx * NT + i
        valid = (lanes8 < keep[0, i]) & (ids < t) & (ids != t - slash[0, 0]) & (ids != t - near)
        flag = jnp.where(valid | (lanes8 >= NV), 0.0, 1.0)
        return jnp.broadcast_to(flag[:1], (ROWS, HD)).astype(BF16)

    for g in range(NG):
        arrived(g, 4)
        for jj in range(G):
            kvert[g, jj] = jnp.concatenate([full[g, p, jj] for p in range(8)], axis=0)
            vvert[g, jj] = jnp.concatenate([full[g, 8 + p, jj] for p in range(8)], axis=0)
        bias = jnp.where(slot_row + g * G == slot_lane, HIDE, 0.0).astype(BF16)

        def vertical(i, _):
            keys = kvert[g].reshape(G * TILE, HD)
            values = vvert[g].reshape(G * TILE, HD)
            query = jnp.concatenate([stacked(i), flags(i)], axis=1)
            scores = dot_nt(query, jnp.concatenate([keys, bias], axis=1))
            top, weights = soft(scores)
            ebuf_b[g, i] = weights
            mx[g + 1, i] = jnp.broadcast_to(top, (ROWS, HD))
            acc[g + 1, i] = mixed(weights, values)
            return 0

        lax.fori_loop(0, NT, vertical, 0, unroll=4)

    slash_copies[1].wait_recv()

    lane_id = lax.broadcasted_iota(jnp.int32, (ROWS, HD), 1)
    win_row = lax.broadcasted_iota(jnp.int32, (2 * NT, TILE), 0)
    vs_row = lax.broadcasted_iota(jnp.int32, (NV, TILE), 0)

    def finish(i, _):
        values = jnp.concatenate([vw[NT + i], vw[i], vw[NT + i - near]], axis=0)
        acc[0, i] = mixed(ebuf_a[i], values)
        tops = [mx[x, i] for x in range(NG + 1)]
        top = functools.reduce(jnp.maximum, tops)
        scales = [jnp.exp2((t - top) * RATE) for t in tops]
        inverse = 1.0 / sum(acc[x, i, :, HD:] * scales[x] for x in range(NG + 1))
        scales = [f * inverse for f in scales]
        for x in range(NG + 1):
            mx[x, i] = scales[x]
        factors = scales[0]
        for x in range(1, NG + 1):
            factors = jnp.where(lane_id == x, scales[x], factors)
        turned = jnp.transpose(factors)[:8]
        high = turned.astype(BF16)
        low = (turned - high.astype(F32)).astype(BF16)
        rows = jnp.concatenate([high, low], axis=0)

        def sums(weights, which):
            both = jnp.dot(rows, weights, preferred_element_type=F32)
            return both[which:which + 1] + both[8 + which:9 + which]

        near_sums = sums(ebuf_a[i], 0)
        add = jnp.where(win_row == NT + i, near_sums[:, :TILE], 0.0)
        add = add + jnp.where(win_row == i, near_sums[:, TILE:2 * TILE], 0.0)
        add = add + jnp.where(win_row == NT + i - near, near_sums[:, 2 * TILE:], 0.0)
        win[...] += add
        total = vs[...]
        for g in range(NG):
            part = sums(ebuf_b[g, i], g + 1)
            for jj in range(G):
                total = total + jnp.where(vs_row == g * G + jj, part[:, jj * TILE:(jj + 1) * TILE], 0.0)
        vs[...] = total
        return 0

    lax.fori_loop(0, NT, finish, 0, unroll=4)

    to_before = remote(win.at[pl.ds(0, NT)], rw, h_s.at[7], h_r.at[7], before)
    to_before.start()
    v1[y] = vs[...]
    c1 = [remote(vs, v1.at[y], t_s.at[n], t_r.at[n], p) for n, (_, p) in enumerate(y_peers)]
    for c in c1:
        c.start()

    def normalise(i, _):
        out = sum(acc[x, i, :, :HD] * mx[x, i] for x in range(NG + 1)).astype(BF16)
        here = pl.ds(pl.multiple_of(i * TILE, TILE), TILE)
        att[here, :] = jnp.concatenate([out[h * TILE:(h + 1) * TILE] for h in range(QPK)], axis=1)
        return 0

    to_before.wait_recv()
    hr[head] = win[NT:] + rw[...]
    ch = [remote(hr.at[head], hr.at[head], h_s.at[n], h_r.at[n], p) for n, (_, p) in enumerate(heads)]
    for c in ch:
        c.start()
    lax.fori_loop(0, NT // 2, normalise, 0)
    for c in c1:
        c.wait_recv()
    v2[zl] = (v1[0] + v1[1]) + (v1[2] + v1[3])
    c2 = [remote(v2.at[zl], v2.at[zl], t_s.at[3 + n], t_r.at[3 + n], p) for n, (_, p) in enumerate(l_peers)]
    for c in c2:
        c.start()
    lax.fori_loop(NT // 2, NT, normalise, 0)
    for c in c2:
        c.wait_recv()
    v3[zh] = (v2[0] + v2[1]) + (v2[2] + v2[3])
    c3 = [remote(v3.at[zh], v3.at[zh], t_s.at[6 + n], t_r.at[6 + n], p) for n, (_, p) in enumerate(h_peers)]
    for c in c3:
        c.start()
    for c in ch:
        c.wait_recv()
    total = hr[0]
    for n in range(1, HEADS):
        total = total + hr[n]
    col_ref[...] = total * (1.0 / (HEADS * QPK))
    for c in c3:
        c.wait_recv()
    ver_ref[0] = ((v3[0] + v3[1]) + (v3[2] + v3[3])) * (1.0 / QPK)

    for c in [c for group in steps.values() for c in group] + slash_copies + [to_before] + c1 + c2 + c3 + ch:
        c.wait_send()


def local(queries, keys, values, vertical_ids, slash_offsets, keep_counts):
    rows = keys.shape[0]
    smem = pl.BlockSpec(memory_space=pltpu.SMEM)
    vmem = pl.BlockSpec(memory_space=pltpu.VMEM)
    hbm = pl.BlockSpec(memory_space=pl.ANY)
    dma = pltpu.SemaphoreType.DMA
    attended, column, vertical = pl.pallas_call(
        kernel,
        out_shape=(
            pltpu.VMEM(queries.shape, BF16),
            pltpu.VMEM((NT, TILE), F32),
            pltpu.VMEM((1, NV, TILE), F32),
        ),
        in_specs=[smem, smem, smem, hbm, hbm, hbm],
        out_specs=(vmem, vmem, vmem),
        scratch_shapes=[
            pltpu.VMEM((rows, QPK * HD), BF16),
            *[pltpu.VMEM((NT, TILE, HD), BF16) for _ in range(2)],
            *[pltpu.VMEM((2 * NT, TILE, HD), BF16) for _ in range(2)],
            *[pltpu.VMEM((NG, G, TILE, HD), BF16) for _ in range(2)],
            pltpu.VMEM((ROWS, HD), BF16),
            pltpu.VMEM((NT, ROWS, 3 * TILE), BF16),
            pltpu.VMEM((NG, NT, ROWS, G * TILE), BF16),
            pltpu.VMEM((NG + 1, NT, ROWS, HD), F32),
            pltpu.VMEM((NG + 1, NT, ROWS, 2 * HD), F32),
            pltpu.VMEM((2 * NT, TILE), F32),
            pltpu.VMEM((NV, TILE), F32),
            pltpu.VMEM((NG, 4, G, 64, HD), BF16),
            *[pltpu.VMEM((NY, G, 64, HD), BF16) for _ in range(2)],
            pltpu.VMEM((NG, NL, G, 16, HD), BF16),
            *[pltpu.VMEM((NL, G, 16, HD), BF16) for _ in range(2)],
            pltpu.VMEM((NG, G, 16, HD), BF16),
            *[pltpu.VMEM((NH, G, 16, HD), BF16) for _ in range(2)],
            pltpu.VMEM((NG, 16, G, 16, HD), BF16),
            pltpu.VMEM((HEADS, NT, TILE), F32),
            pltpu.VMEM((NT, TILE), F32),
            pltpu.VMEM((NY, NV, TILE), F32),
            pltpu.VMEM((NL, NV, TILE), F32),
            pltpu.VMEM((NH, NV, TILE), F32),
            dma((5,)), dma((2,)), dma((2,)),
            dma((NG * 15,)), dma((NG * 15,)), dma((12,)), dma((12,)), dma((9,)), dma((9,)), dma((8,)), dma((8,)),
        ],
        compiler_params=pltpu.CompilerParams(
            collective_id=0, has_side_effects=True, vmem_limit_bytes=56 << 20
        ),
    )(vertical_ids, slash_offsets, keep_counts, queries, keys.reshape(NT, TILE, HD), values.reshape(NT, TILE, HD))
    return attended, column.reshape(rows), vertical


def solution(mesh):
    placed = (
        P("ctx", "head"),
        P("ctx", "head"),
        P("ctx", "head"),
        P("head", None),
        P("head", None),
        P("head", "ctx"),
    )
    return jax.shard_map(
        local,
        mesh=mesh,
        in_specs=placed,
        out_specs=(P("ctx", "head"), P("ctx"), P("head", None, None)),
        check_vma=False,
    )
```

```python
import functools
import math

import jax
import jax.numpy as jnp
from jax import lax
from jax.experimental import pallas as pl
from jax.experimental.pallas import tpu as pltpu
from jax.sharding import PartitionSpec as P

MESH = pl.DeviceIdType.MESH
QPK = 4
TILE = 128
HD = 128
NV = 8
NT = 8
ROWS = QPK * TILE
NG = 2
G = NV // NG
NY = 4
NL = 4
NH = 4
HEADS = 8
CTX = NY * NL * NH
HIDE = -1e30
RATE = HD ** -0.5 * math.log2(math.e)
NEAR = (-1, -2, 1)
SLASH_K = 0
SLASH_V = 2
F32 = jnp.float32
BF16 = jnp.bfloat16


def dot_nt(a, b):
    return lax.dot_general(a, b, (((1,), (1,)), ((), ())), preferred_element_type=F32)


def kernel(vert, slash, keep, q_hbm, k_hbm, v_hbm, att, col_ref, ver_ref,
           q, ko, vo, kw, vw, kvert, vvert, causal, ebuf_a, ebuf_b, mx, acc0, acc, sc, win, vs,
           s1, r1a, r1b, s2, r2a, r2b, s3, r3a, r3b, full,
           hr, rw, v1, vz,
           in_sem, slash_s, slash_r, ex_s, ex_r, t_s, t_r, h_s, h_r):
    head = lax.axis_index("head")
    ctx = lax.axis_index("ctx")
    y = ctx // (NL * NH)
    zh = (ctx // NL) % NH
    zl = ctx % NL
    z = ctx % (NL * NH)

    def at(a, b, c):
        return (head, a * (NL * NH) + b * NL + c)

    def along(k):
        return (head, y * (NL * NH) + (z + k + NL * NH) % (NL * NH))

    y_peers = [((y + k) % NY, at((y + k) % NY, zh, zl)) for k in (1, 2, 3)]
    h_peers = [((zh + k) % NH, at(y, (zh + k) % NH, zl)) for k in (1, 2, 3)]
    n_peers = [((zl + k + NL) % NL, along(k)) for k in NEAR]
    heads = [((head + k) % HEADS, ((head + k) % HEADS, ctx)) for k in range(1, HEADS)]
    after = (head, (ctx + 1) % CTX)
    before = (head, (ctx + CTX - 1) % CTX)

    barrier = pltpu.get_barrier_semaphore()
    z_peers = [along(k) for k in (8, 7, -7, 6, -6, 5, -5, 4, -4, 3, -3, 2, -2, 1, -1)]
    greeted = z_peers + [p for _, p in y_peers + heads] + [after, before]
    for p in greeted:
        pl.semaphore_signal(barrier, inc=1, device_id=p, device_id_type=MESH)

    loads = [
        pltpu.make_async_copy(k_hbm, ko, in_sem.at[0]),
        pltpu.make_async_copy(v_hbm, vo, in_sem.at[1]),
        pltpu.make_async_copy(q_hbm, q, in_sem.at[2]),
        pltpu.make_async_copy(k_hbm, kw.at[pl.ds(NT, NT)], in_sem.at[3]),
        pltpu.make_async_copy(v_hbm, vw.at[pl.ds(NT, NT)], in_sem.at[4]),
    ]
    for c in loads:
        c.start()

    def remote(src, dst, ss, rs, p):
        return pltpu.make_async_remote_copy(
            src_ref=src, dst_ref=dst, send_sem=ss, recv_sem=rs, device_id=p, device_id_type=MESH
        )

    row = lax.broadcasted_iota(jnp.int32, (ROWS, HD), 0) % TILE
    lane = lax.broadcasted_iota(jnp.int32, (ROWS, HD), 1)
    causal[...] = jnp.where((lane == 0) | (lane > row), 1.0, 0.0).astype(BF16)

    loads[0].wait()
    loads[1].wait()
    for j in range(NV):
        g, jj = divmod(j, G)
        for part, ref in ((0, ko), (1, vo)):
            tile = ref[vert[0, j] & (NT - 1)]
            for piece in range(8):
                of_y, of_l = divmod(8 * part + piece, NL)
                rows = tile[16 * piece:16 * piece + 16]
                if g == 0:
                    s1[g, of_y, jj, 16 * of_l:16 * of_l + 16] = rows
                else:
                    s1[g, of_l, jj, 16 * of_y:16 * of_y + 16] = rows
    r1 = (r1a, r1b)
    r2 = (r2a, r2b)
    r3 = (r3a, r3b)
    mine = ((y, zl), (zl, y))
    peers = ((y_peers, n_peers), (n_peers, y_peers))
    for g in range(NG):
        r1[g][mine[g][0]] = s1[g, mine[g][0]]

    pl.semaphore_wait(barrier, len(greeted))

    def stage(g, number, peers, src, dst):
        base = (g * 5 + number) * 3
        return [
            remote(src(i), dst(i), ex_s.at[base + n], ex_r.at[base + n], p)
            for n, (i, p) in enumerate(peers)
        ]

    steps = {}
    for g in range(NG):
        steps[g, 0] = stage(g, 0, peers[g][0], lambda i: s1.at[g, i], lambda i: r1[g].at[mine[g][0]])
        for c in steps[g, 0]:
            c.start()
    lower = pl.ds(0, NT)
    slash_copies = [
        remote(ko, kw.at[lower], slash_s.at[0], slash_r.at[0], after),
        remote(vo, vw.at[lower], slash_s.at[1], slash_r.at[1], after),
    ]

    def send_slash(number):
        for c, when in zip(slash_copies, (SLASH_K, SLASH_V)):
            if when == number:
                c.start()

    send_slash(0)

    def owner(j, low, count):
        return (vert[0, j] >> low) & (count - 1)

    def arrived(g, number):
        for c in steps[g, number]:
            c.wait_recv()

    for g in range(NG):
        arrived(g, 0)
        for jj in range(G):
            j = g * G + jj
            src = owner(j, 7, NY) if g == 0 else owner(j, 3, NL)
            block = r1[g][src, jj]
            for n in range(4):
                s2[g, n, jj] = block[16 * n:16 * n + 16]
        r2[g][mine[g][1]] = s2[g, mine[g][1]]
        steps[g, 1] = stage(g, 1, peers[g][1], lambda i: s2.at[g, i], lambda i: r2[g].at[mine[g][1]])
        for c in steps[g, 1]:
            c.start()
    send_slash(1)
    for g in range(NG):
        arrived(g, 1)
        for jj in range(G):
            j = g * G + jj
            src = owner(j, 3, NL) if g == 0 else owner(j, 7, NY)
            s3[g, jj] = r2[g][src, jj]
        r3[g][zh] = s3[g]
        steps[g, 2] = stage(g, 2, h_peers, lambda i: s3.at[g], lambda i: r3[g].at[zh])
        for c in steps[g, 2]:
            c.start()
    send_slash(2)

    for c in loads[2:]:
        c.wait()
    slash_copies[0].wait_recv()
    key_row = lax.broadcasted_iota(jnp.int32, (TILE, HD), 0)
    key_lane = lax.broadcasted_iota(jnp.int32, (TILE, HD), 1)
    near = slash[0, 1]

    def stacked(i):
        rows = q[pl.ds(pl.multiple_of(i * TILE, TILE), TILE), :]
        return jnp.concatenate([rows[:, h * HD:(h + 1) * HD] for h in range(QPK)], axis=0)

    def soft(scores):
        top = jnp.max(scores, axis=1, keepdims=True)
        return top, jnp.exp2((scores - top) * RATE).astype(BF16)

    def mixed(weights, value_rows):
        ones = jnp.ones(value_rows.shape, BF16)
        return jnp.dot(weights, jnp.concatenate([value_rows, ones], axis=1), preferred_element_type=F32)

    def first(i, _):
        t = ctx * NT + i
        keys = jnp.concatenate([kw[NT + i], kw[i], kw[NT + i - near]], axis=0)
        diagonal = jnp.where((key_row == key_lane) & (key_lane > 0), HIDE, 0.0).astype(BF16)
        far_bias = jnp.where((key_lane == 0) & (key_lane + t < slash[0, 0]), HIDE, 0.0).astype(BF16)
        near_bias = jnp.where((key_lane == 0) & (key_lane + t < near), HIDE, 0.0).astype(BF16)
        bias = jnp.concatenate([diagonal, far_bias, near_bias], axis=0)
        query = jnp.concatenate([stacked(i), causal[...]], axis=1)
        scores = dot_nt(query, jnp.concatenate([keys, bias], axis=1))
        top, weights = soft(scores)
        ebuf_a[i] = weights
        mx[0, i] = jnp.broadcast_to(top, (ROWS, HD))
        return 0

    lax.fori_loop(0, NT, first, 0, unroll=4)

    piece = (4 * y + zl, 4 * zl + y)
    for g in range(NG):
        arrived(g, 2)
        for jj in range(G):
            j = g * G + jj
            of = owner(j, 3, NL * NH)
            gathered = (of + ((zl - of + 2) & (NL - 1)) - 2) & (NL * NH - 1)
            full[g, piece[g], jj] = r3[g][gathered >> 2, jj]
        steps[g, 3] = stage(g, 3, peers[g][1], lambda i: full.at[g, piece[g]], lambda i: full.at[g, piece[g]])
        for c in steps[g, 3]:
            c.start()
    send_slash(3)
    for g in range(NG):
        arrived(g, 3)
        block = pl.ds(4 * mine[g][0], 4)
        steps[g, 4] = stage(g, 4, peers[g][0], lambda i: full.at[g, block], lambda i: full.at[g, block])
        for c in steps[g, 4]:
            c.start()
    send_slash(4)

    slash_copies[1].wait_recv()

    def mix(i, _):
        values = jnp.concatenate([vw[NT + i], vw[i], vw[NT + i - near]], axis=0)
        acc0[i] = mixed(ebuf_a[i], values)
        return 0

    lax.fori_loop(0, NT, mix, 0, unroll=4)

    lanes8 = lax.broadcasted_iota(jnp.int32, (8, HD), 1)
    ids = jnp.zeros((8, HD), jnp.int32)
    for j in range(NV):
        ids = jnp.where(lanes8 == j, vert[0, j], ids)
    slot_row = lax.broadcasted_iota(jnp.int32, (G * TILE, HD), 0) // TILE
    slot_lane = lax.broadcasted_iota(jnp.int32, (G * TILE, HD), 1)

    def flags(i):
        t = ctx * NT + i
        valid = (lanes8 < keep[0, i]) & (ids < t) & (ids != t - slash[0, 0]) & (ids != t - near)
        flag = jnp.where(valid | (lanes8 >= NV), 0.0, 1.0)
        return jnp.broadcast_to(flag[:1], (ROWS, HD)).astype(BF16)

    for g in range(NG):
        arrived(g, 4)
        for jj in range(G):
            order = [p if g == 0 else 4 * (p % 4) + p // 4 for p in range(16)]
            kvert[g, jj] = jnp.concatenate([full[g, p, jj] for p in order[:8]], axis=0)
            vvert[g, jj] = jnp.concatenate([full[g, p, jj] for p in order[8:]], axis=0)
        bias = jnp.where(slot_row + g * G == slot_lane, HIDE, 0.0).astype(BF16)

        def vertical(i, _):
            keys = kvert[g].reshape(G * TILE, HD)
            values = vvert[g].reshape(G * TILE, HD)
            query = jnp.concatenate([stacked(i), flags(i)], axis=1)
            scores = dot_nt(query, jnp.concatenate([keys, bias], axis=1))
            top, weights = soft(scores)
            ebuf_b[g, i] = weights
            mx[g + 1, i] = jnp.broadcast_to(top, (ROWS, HD))
            acc[g, i] = mixed(weights, values)
            return 0

        lax.fori_loop(0, NT, vertical, 0, unroll=8)

    lane_id = lax.broadcasted_iota(jnp.int32, (ROWS, HD), 1)
    win_row = lax.broadcasted_iota(jnp.int32, (2 * NT, TILE), 0)
    vs_row = lax.broadcasted_iota(jnp.int32, (NV, TILE), 0)

    def finish(i, carry):
        window_sums, vertical_sums = carry
        tops = [mx[x, i] for x in range(NG + 1)]
        top = functools.reduce(jnp.maximum, tops)
        scales = [jnp.exp2((t - top) * RATE) for t in tops]
        total = acc0[i, :, HD:] * scales[0]
        for g in range(NG):
            total = total + acc[g, i, :, HD:] * scales[g + 1]
        inverse = 1.0 / total
        scales = [f * inverse for f in scales]
        for x in range(NG + 1):
            sc[x, i] = scales[x]
        factors = scales[0]
        for x in range(1, NG + 1):
            factors = jnp.where(lane_id == x, scales[x], factors)
        turned = jnp.transpose(factors)[:8]
        high = turned.astype(BF16)
        low = (turned - high.astype(F32)).astype(BF16)
        rows = jnp.concatenate([high, low], axis=0)

        def sums(weights, which):
            both = jnp.dot(rows, weights, preferred_element_type=F32)
            return both[which:which + 1] + both[8 + which:9 + which]

        near_sums = sums(ebuf_a[i], 0)
        add = jnp.where(win_row == NT + i, near_sums[:, :TILE], 0.0)
        add = add + jnp.where(win_row == i, near_sums[:, TILE:2 * TILE], 0.0)
        add = add + jnp.where(win_row == NT + i - near, near_sums[:, 2 * TILE:], 0.0)
        for g in range(NG):
            part = sums(ebuf_b[g, i], g + 1)
            for jj in range(G):
                here = vs_row == g * G + jj
                vertical_sums = vertical_sums + jnp.where(here, part[:, jj * TILE:(jj + 1) * TILE], 0.0)
        return window_sums + add, vertical_sums

    zeros = (jnp.zeros((2 * NT, TILE), F32), jnp.zeros((NV, TILE), F32))
    win[...], vs[...] = lax.fori_loop(0, NT, finish, zeros, unroll=8)

    to_before = remote(win.at[pl.ds(0, NT)], rw, h_s.at[7], h_r.at[7], before)
    to_before.start()
    v1[y] = vs[...]
    c1 = [remote(vs, v1.at[y], t_s.at[n], t_r.at[n], p) for n, (_, p) in enumerate(y_peers)]
    for c in c1:
        c.start()

    def normalise(i, _):
        out = acc0[i, :, :HD] * sc[0, i]
        for g in range(NG):
            out = out + acc[g, i, :, :HD] * sc[g + 1, i]
        out = out.astype(BF16)
        here = pl.ds(pl.multiple_of(i * TILE, TILE), TILE)
        att[here, :] = jnp.concatenate([out[h * TILE:(h + 1) * TILE] for h in range(QPK)], axis=1)
        return 0

    to_before.wait_recv()
    hr[head] = win[NT:] + rw[...]
    ch = [remote(hr.at[head], hr.at[head], h_s.at[n], h_r.at[n], p) for n, (_, p) in enumerate(heads)]
    for c in ch:
        c.start()
    lax.fori_loop(0, NT // 2, normalise, 0)
    for c in c1:
        c.wait_recv()
    vz[z] = (v1[0] + v1[1]) + (v1[2] + v1[3])
    c2 = [remote(vz.at[z], vz.at[z], t_s.at[3 + n], t_r.at[3 + n], p) for n, p in enumerate(z_peers)]
    for c in c2:
        c.start()
    lax.fori_loop(NT // 2, NT, normalise, 0)
    for c in ch:
        c.wait_recv()
    total = hr[0]
    for n in range(1, HEADS):
        total = total + hr[n]
    col_ref[...] = total * (1.0 / (HEADS * QPK))
    for c in [c for group in steps.values() for c in group] + slash_copies + [to_before] + c1:
        c.wait_send()
    for c in c2:
        c.wait_recv()
    total = vz[0]
    for n in range(1, NL * NH):
        total = total + vz[n]
    ver_ref[0] = total * (1.0 / QPK)

    for c in c2 + ch:
        c.wait_send()


def local(queries, keys, values, vertical_ids, slash_offsets, keep_counts):
    rows = keys.shape[0]
    smem = pl.BlockSpec(memory_space=pltpu.SMEM)
    vmem = pl.BlockSpec(memory_space=pltpu.VMEM)
    hbm = pl.BlockSpec(memory_space=pl.ANY)
    dma = pltpu.SemaphoreType.DMA
    attended, column, vertical = pl.pallas_call(
        kernel,
        out_shape=(
            pltpu.VMEM(queries.shape, BF16),
            pltpu.VMEM((NT, TILE), F32),
            pltpu.VMEM((1, NV, TILE), F32),
        ),
        in_specs=[smem, smem, smem, hbm, hbm, hbm],
        out_specs=(vmem, vmem, vmem),
        scratch_shapes=[
            pltpu.VMEM((rows, QPK * HD), BF16),
            *[pltpu.VMEM((NT, TILE, HD), BF16) for _ in range(2)],
            *[pltpu.VMEM((2 * NT, TILE, HD), BF16) for _ in range(2)],
            *[pltpu.VMEM((NG, G, TILE, HD), BF16) for _ in range(2)],
            pltpu.VMEM((ROWS, HD), BF16),
            pltpu.VMEM((NT, ROWS, 3 * TILE), BF16),
            pltpu.VMEM((NG, NT, ROWS, G * TILE), BF16),
            pltpu.VMEM((NG + 1, NT, ROWS, HD), F32),
            pltpu.VMEM((NT, ROWS, 2 * HD), F32),
            pltpu.VMEM((NG, NT, ROWS, 2 * HD), F32),
            pltpu.VMEM((NG + 1, NT, ROWS, HD), F32),
            pltpu.VMEM((2 * NT, TILE), F32),
            pltpu.VMEM((NV, TILE), F32),
            pltpu.VMEM((NG, 4, G, 64, HD), BF16),
            *[pltpu.VMEM((NY, G, 64, HD), BF16) for _ in range(2)],
            pltpu.VMEM((NG, NL, G, 16, HD), BF16),
            *[pltpu.VMEM((NL, G, 16, HD), BF16) for _ in range(2)],
            pltpu.VMEM((NG, G, 16, HD), BF16),
            *[pltpu.VMEM((NH, G, 16, HD), BF16) for _ in range(2)],
            pltpu.VMEM((NG, 16, G, 16, HD), BF16),
            pltpu.VMEM((HEADS, NT, TILE), F32),
            pltpu.VMEM((NT, TILE), F32),
            pltpu.VMEM((NY, NV, TILE), F32),
            pltpu.VMEM((NL * NH, NV, TILE), F32),
            dma((5,)), dma((2,)), dma((2,)),
            dma((NG * 15,)), dma((NG * 15,)), dma((18,)), dma((18,)), dma((8,)), dma((8,)),
        ],
        compiler_params=pltpu.CompilerParams(
            collective_id=0, has_side_effects=True, vmem_limit_bytes=56 << 20
        ),
    )(vertical_ids, slash_offsets, keep_counts, queries, keys.reshape(NT, TILE, HD), values.reshape(NT, TILE, HD))
    return attended, column.reshape(rows), vertical


def solution(mesh):
    placed = (
        P("ctx", "head"),
        P("ctx", "head"),
        P("ctx", "head"),
        P("head", None),
        P("head", None),
        P("head", "ctx"),
    )
    return jax.shard_map(
        local,
        mesh=mesh,
        in_specs=placed,
        out_specs=(P("ctx", "head"), P("ctx"), P("head", None, None)),
        check_vma=False,
    )
```

```python
import functools
import math

import jax
import jax.numpy as jnp
from jax import lax
from jax.experimental import pallas as pl
from jax.experimental.pallas import tpu as pltpu
from jax.sharding import PartitionSpec as P

MESH = pl.DeviceIdType.MESH
QPK = 4
TILE = 128
HD = 128
NV = 8
NT = 8
ROWS = QPK * TILE
NG = 2
G = NV // NG
NY = 4
NL = 4
NH = 4
HEADS = 8
CTX = NY * NL * NH
HIDE = -1e30
RATE = HD ** -0.5 * math.log2(math.e)
NEAR = (-1, -2, 1)
SLASH_K = 1
SLASH_V = 2
F32 = jnp.float32
BF16 = jnp.bfloat16


def dot_nt(a, b):
    return lax.dot_general(a, b, (((1,), (1,)), ((), ())), preferred_element_type=F32)


def kernel(vert_hbm, slash_hbm, keep_hbm, q_hbm, k_hbm, v_hbm, att, col_ref, ver_ref,
           vert, slash, keep, q, ko, vo, kw, vw, kvert, vvert, causal, ebuf_a, ebuf_b, mx, acc0, acc, sc, win, vs,
           s1, r1a, r1b, s2, r2a, r2b, s3, r3a, r3b, full,
           hr, rw, v1, vz,
           in_sem, slash_s, slash_r, ex_s, ex_r, t_s, t_r, h_s, h_r):
    head = lax.axis_index("head")
    ctx = lax.axis_index("ctx")
    y = ctx // (NL * NH)
    zh = (ctx // NL) % NH
    zl = ctx % NL
    z = ctx % (NL * NH)

    def at(a, b, c):
        return (head, a * (NL * NH) + b * NL + c)

    def along(k):
        return (head, y * (NL * NH) + (z + k + NL * NH) % (NL * NH))

    y_peers = [((y + k) % NY, at((y + k) % NY, zh, zl)) for k in (1, 2, 3)]
    h_peers = [((zh + k) % NH, at(y, (zh + k) % NH, zl)) for k in (1, 2, 3)]
    n_peers = [((zl + k + NL) % NL, along(k)) for k in NEAR]
    heads = [((head + k) % HEADS, ((head + k) % HEADS, ctx)) for k in range(1, HEADS)]
    after = (head, (ctx + 1) % CTX)
    before = (head, (ctx + CTX - 1) % CTX)

    barrier = pltpu.get_barrier_semaphore()
    z_peers = [along(k) for k in (8, 7, -7, 6, -6, 5, -5, 4, -4, 3, -3, 2, -2, 1, -1)]
    greeted = z_peers + [p for _, p in y_peers + heads] + [after, before]
    for p in greeted:
        pl.semaphore_signal(barrier, inc=1, device_id=p, device_id_type=MESH)

    loads = [
        pltpu.make_async_copy(k_hbm, ko, in_sem.at[0]),
        pltpu.make_async_copy(v_hbm, vo, in_sem.at[1]),
        pltpu.make_async_copy(q_hbm, q, in_sem.at[2]),
        pltpu.make_async_copy(k_hbm, kw.at[pl.ds(NT, NT)], in_sem.at[3]),
        pltpu.make_async_copy(v_hbm, vw.at[pl.ds(NT, NT)], in_sem.at[4]),
    ]
    small = [
        pltpu.make_async_copy(vert_hbm, vert, in_sem.at[5]),
        pltpu.make_async_copy(slash_hbm, slash, in_sem.at[6]),
        pltpu.make_async_copy(keep_hbm, keep, in_sem.at[7]),
    ]
    for c in small + loads:
        c.start()

    def remote(src, dst, ss, rs, p):
        return pltpu.make_async_remote_copy(
            src_ref=src, dst_ref=dst, send_sem=ss, recv_sem=rs, device_id=p, device_id_type=MESH
        )

    row = lax.broadcasted_iota(jnp.int32, (ROWS, HD), 0) % TILE
    lane = lax.broadcasted_iota(jnp.int32, (ROWS, HD), 1)
    causal[...] = jnp.where((lane == 0) | (lane > row), 1.0, 0.0).astype(BF16)

    for c in small + loads[:2]:
        c.wait()
    for j in range(NV):
        g, jj = divmod(j, G)
        for part, ref in ((0, ko), (1, vo)):
            tile = ref[vert[0, j] & (NT - 1)]
            for piece in range(8):
                of_y, of_l = divmod(8 * part + piece, NL)
                rows = tile[16 * piece:16 * piece + 16]
                if g == 0:
                    s1[g, of_y, jj, 16 * of_l:16 * of_l + 16] = rows
                else:
                    s1[g, of_l, jj, 16 * of_y:16 * of_y + 16] = rows
    r1 = (r1a, r1b)
    r2 = (r2a, r2b)
    r3 = (r3a, r3b)
    mine = ((y, zl), (zl, y))
    peers = ((y_peers, n_peers), (n_peers, y_peers))
    for g in range(NG):
        r1[g][mine[g][0]] = s1[g, mine[g][0]]

    pl.semaphore_wait(barrier, len(greeted))

    def stage(g, number, peers, src, dst):
        base = (g * 5 + number) * 3
        return [
            remote(src(i), dst(i), ex_s.at[base + n], ex_r.at[base + n], p)
            for n, (i, p) in enumerate(peers)
        ]

    steps = {}
    for g in range(NG):
        steps[g, 0] = stage(g, 0, peers[g][0], lambda i: s1.at[g, i], lambda i: r1[g].at[mine[g][0]])
        for c in steps[g, 0]:
            c.start()
    lower = pl.ds(0, NT)
    slash_copies = [
        remote(ko, kw.at[lower], slash_s.at[0], slash_r.at[0], after),
        remote(vo, vw.at[lower], slash_s.at[1], slash_r.at[1], after),
    ]

    def send_slash(number):
        for c, when in zip(slash_copies, (SLASH_K, SLASH_V)):
            if when == number:
                c.start()

    send_slash(0)

    def owner(j, low, count):
        return (vert[0, j] >> low) & (count - 1)

    def arrived(g, number):
        for c in steps[g, number]:
            c.wait_recv()

    for g in range(NG):
        arrived(g, 0)
        for jj in range(G):
            j = g * G + jj
            src = owner(j, 7, NY) if g == 0 else owner(j, 3, NL)
            block = r1[g][src, jj]
            for n in range(4):
                s2[g, n, jj] = block[16 * n:16 * n + 16]
        r2[g][mine[g][1]] = s2[g, mine[g][1]]
        steps[g, 1] = stage(g, 1, peers[g][1], lambda i: s2.at[g, i], lambda i: r2[g].at[mine[g][1]])
        for c in steps[g, 1]:
            c.start()
    send_slash(1)
    for g in range(NG):
        arrived(g, 1)
        for jj in range(G):
            j = g * G + jj
            src = owner(j, 3, NL) if g == 0 else owner(j, 7, NY)
            s3[g, jj] = r2[g][src, jj]
        r3[g][zh] = s3[g]
        steps[g, 2] = stage(g, 2, h_peers, lambda i: s3.at[g], lambda i: r3[g].at[zh])
        for c in steps[g, 2]:
            c.start()
    send_slash(2)

    piece = (4 * y + zl, 4 * zl + y)
    for g in range(NG):
        arrived(g, 2)
        for jj in range(G):
            j = g * G + jj
            of = owner(j, 3, NL * NH)
            gathered = (of + ((zl - of + 2) & (NL - 1)) - 2) & (NL * NH - 1)
            full[g, piece[g], jj] = r3[g][gathered >> 2, jj]
        steps[g, 3] = stage(g, 3, peers[g][1], lambda i: full.at[g, piece[g]], lambda i: full.at[g, piece[g]])
        for c in steps[g, 3]:
            c.start()
    send_slash(3)
    for g in range(NG):
        arrived(g, 3)
        block = pl.ds(4 * mine[g][0], 4)
        steps[g, 4] = stage(g, 4, peers[g][0], lambda i: full.at[g, block], lambda i: full.at[g, block])
        for c in steps[g, 4]:
            c.start()
    send_slash(4)

    for c in loads[2:]:
        c.wait()
    slash_copies[0].wait_recv()
    key_row = lax.broadcasted_iota(jnp.int32, (TILE, HD), 0)
    key_lane = lax.broadcasted_iota(jnp.int32, (TILE, HD), 1)
    near = slash[0, 1]

    def stacked(i):
        rows = q[pl.ds(pl.multiple_of(i * TILE, TILE), TILE), :]
        return jnp.concatenate([rows[:, h * HD:(h + 1) * HD] for h in range(QPK)], axis=0)

    def soft(scores):
        top = jnp.max(scores, axis=1, keepdims=True)
        return top, jnp.exp2((scores - top) * RATE).astype(BF16)

    def mixed(weights, value_rows):
        ones = jnp.ones(value_rows.shape, BF16)
        return jnp.dot(weights, jnp.concatenate([value_rows, ones], axis=1), preferred_element_type=F32)

    def first(i, _):
        t = ctx * NT + i
        keys = jnp.concatenate([kw[NT + i], kw[i], kw[NT + i - near]], axis=0)
        diagonal = jnp.where((key_row == key_lane) & (key_lane > 0), HIDE, 0.0).astype(BF16)
        far_bias = jnp.where((key_lane == 0) & (key_lane + t < slash[0, 0]), HIDE, 0.0).astype(BF16)
        near_bias = jnp.where((key_lane == 0) & (key_lane + t < near), HIDE, 0.0).astype(BF16)
        bias = jnp.concatenate([diagonal, far_bias, near_bias], axis=0)
        query = jnp.concatenate([stacked(i), causal[...]], axis=1)
        scores = dot_nt(query, jnp.concatenate([keys, bias], axis=1))
        top, weights = soft(scores)
        ebuf_a[i] = weights
        mx[0, i] = jnp.broadcast_to(top, (ROWS, HD))
        return 0

    lax.fori_loop(0, NT, first, 0, unroll=4)

    slash_copies[1].wait_recv()

    def mix(i, _):
        values = jnp.concatenate([vw[NT + i], vw[i], vw[NT + i - near]], axis=0)
        acc0[i] = mixed(ebuf_a[i], values)
        return 0

    lax.fori_loop(0, NT, mix, 0, unroll=4)

    lanes8 = lax.broadcasted_iota(jnp.int32, (8, HD), 1)
    ids = jnp.zeros((8, HD), jnp.int32)
    for j in range(NV):
        ids = jnp.where(lanes8 == j, vert[0, j], ids)
    slot_row = lax.broadcasted_iota(jnp.int32, (G * TILE, HD), 0) // TILE
    slot_lane = lax.broadcasted_iota(jnp.int32, (G * TILE, HD), 1)

    def flags(i):
        t = ctx * NT + i
        valid = (lanes8 < keep[0, i]) & (ids < t) & (ids != t - slash[0, 0]) & (ids != t - near)
        flag = jnp.where(valid | (lanes8 >= NV), 0.0, 1.0)
        return jnp.broadcast_to(flag[:1], (ROWS, HD)).astype(BF16)

    for g in range(NG):
        arrived(g, 4)
        for jj in range(G):
            order = [p if g == 0 else 4 * (p % 4) + p // 4 for p in range(16)]
            kvert[g, jj] = jnp.concatenate([full[g, p, jj] for p in order[:8]], axis=0)
            vvert[g, jj] = jnp.concatenate([full[g, p, jj] for p in order[8:]], axis=0)
        bias = jnp.where(slot_row + g * G == slot_lane, HIDE, 0.0).astype(BF16)

        def vertical(i, _):
            keys = kvert[g].reshape(G * TILE, HD)
            values = vvert[g].reshape(G * TILE, HD)
            query = jnp.concatenate([stacked(i), flags(i)], axis=1)
            scores = dot_nt(query, jnp.concatenate([keys, bias], axis=1))
            top, weights = soft(scores)
            ebuf_b[g, i] = weights
            mx[g + 1, i] = jnp.broadcast_to(top, (ROWS, HD))
            acc[g, i] = mixed(weights, values)
            return 0

        lax.fori_loop(0, NT, vertical, 0, unroll=8)

    lane_id = lax.broadcasted_iota(jnp.int32, (ROWS, HD), 1)
    win_row = lax.broadcasted_iota(jnp.int32, (2 * NT, TILE), 0)
    vs_row = lax.broadcasted_iota(jnp.int32, (NV, TILE), 0)

    def finish(i, carry):
        window_sums, vertical_sums = carry
        tops = [mx[x, i] for x in range(NG + 1)]
        top = functools.reduce(jnp.maximum, tops)
        scales = [jnp.exp2((t - top) * RATE) for t in tops]
        total = acc0[i, :, HD:] * scales[0]
        for g in range(NG):
            total = total + acc[g, i, :, HD:] * scales[g + 1]
        inverse = 1.0 / total
        scales = [f * inverse for f in scales]
        for x in range(NG + 1):
            sc[x, i] = scales[x]
        factors = scales[0]
        for x in range(1, NG + 1):
            factors = jnp.where(lane_id == x, scales[x], factors)
        turned = jnp.transpose(factors)[:8]
        high = turned.astype(BF16)
        low = (turned - high.astype(F32)).astype(BF16)
        rows = jnp.concatenate([high, low], axis=0)

        def sums(weights, which):
            both = jnp.dot(rows, weights, preferred_element_type=F32)
            return both[which:which + 1] + both[8 + which:9 + which]

        near_sums = sums(ebuf_a[i], 0)
        add = jnp.where(win_row == NT + i, near_sums[:, :TILE], 0.0)
        add = add + jnp.where(win_row == i, near_sums[:, TILE:2 * TILE], 0.0)
        add = add + jnp.where(win_row == NT + i - near, near_sums[:, 2 * TILE:], 0.0)
        for g in range(NG):
            part = sums(ebuf_b[g, i], g + 1)
            for jj in range(G):
                here = vs_row == g * G + jj
                vertical_sums = vertical_sums + jnp.where(here, part[:, jj * TILE:(jj + 1) * TILE], 0.0)
        return window_sums + add, vertical_sums

    zeros = (jnp.zeros((2 * NT, TILE), F32), jnp.zeros((NV, TILE), F32))
    win[...], vs[...] = lax.fori_loop(0, NT, finish, zeros, unroll=8)

    to_before = remote(win.at[pl.ds(0, NT)], rw, h_s.at[7], h_r.at[7], before)
    to_before.start()
    v1[y] = vs[...]
    c1 = [remote(vs, v1.at[y], t_s.at[n], t_r.at[n], p) for n, (_, p) in enumerate(y_peers)]
    for c in c1:
        c.start()

    def normalise(i, _):
        out = acc0[i, :, :HD] * sc[0, i]
        for g in range(NG):
            out = out + acc[g, i, :, :HD] * sc[g + 1, i]
        out = out.astype(BF16)
        here = pl.ds(pl.multiple_of(i * TILE, TILE), TILE)
        att[here, :] = jnp.concatenate([out[h * TILE:(h + 1) * TILE] for h in range(QPK)], axis=1)
        return 0

    to_before.wait_recv()
    hr[head] = win[NT:] + rw[...]
    ch = [remote(hr.at[head], hr.at[head], h_s.at[n], h_r.at[n], p) for n, (_, p) in enumerate(heads)]
    for c in ch:
        c.start()
    lax.fori_loop(0, NT // 2, normalise, 0)
    for c in c1:
        c.wait_recv()
    vz[z] = (v1[0] + v1[1]) + (v1[2] + v1[3])
    c2 = [remote(vz.at[z], vz.at[z], t_s.at[3 + n], t_r.at[3 + n], p) for n, p in enumerate(z_peers)]
    for c in c2:
        c.start()
    lax.fori_loop(NT // 2, NT, normalise, 0)
    for c in ch:
        c.wait_recv()
    total = hr[0]
    for n in range(1, HEADS):
        total = total + hr[n]
    col_ref[...] = total * (1.0 / (HEADS * QPK))
    for c in [c for group in steps.values() for c in group] + slash_copies + [to_before] + c1:
        c.wait_send()
    for c in c2:
        c.wait_recv()
    total = vz[0]
    for n in range(1, NL * NH):
        total = total + vz[n]
    ver_ref[0] = total * (1.0 / QPK)

    for c in c2 + ch:
        c.wait_send()


def local(queries, keys, values, vertical_ids, slash_offsets, keep_counts):
    rows = keys.shape[0]
    vmem = pl.BlockSpec(memory_space=pltpu.VMEM)
    hbm = pl.BlockSpec(memory_space=pl.ANY)
    dma = pltpu.SemaphoreType.DMA
    attended, column, vertical = pl.pallas_call(
        kernel,
        out_shape=(
            pltpu.VMEM(queries.shape, BF16),
            pltpu.VMEM((NT, TILE), F32),
            pltpu.VMEM((1, NV, TILE), F32),
        ),
        in_specs=[hbm] * 6,
        out_specs=(vmem, vmem, vmem),
        scratch_shapes=[
            *[pltpu.SMEM(a.shape, jnp.int32) for a in (vertical_ids, slash_offsets, keep_counts)],
            pltpu.VMEM((rows, QPK * HD), BF16),
            *[pltpu.VMEM((NT, TILE, HD), BF16) for _ in range(2)],
            *[pltpu.VMEM((2 * NT, TILE, HD), BF16) for _ in range(2)],
            *[pltpu.VMEM((NG, G, TILE, HD), BF16) for _ in range(2)],
            pltpu.VMEM((ROWS, HD), BF16),
            pltpu.VMEM((NT, ROWS, 3 * TILE), BF16),
            pltpu.VMEM((NG, NT, ROWS, G * TILE), BF16),
            pltpu.VMEM((NG + 1, NT, ROWS, HD), F32),
            pltpu.VMEM((NT, ROWS, 2 * HD), F32),
            pltpu.VMEM((NG, NT, ROWS, 2 * HD), F32),
            pltpu.VMEM((NG + 1, NT, ROWS, HD), F32),
            pltpu.VMEM((2 * NT, TILE), F32),
            pltpu.VMEM((NV, TILE), F32),
            pltpu.VMEM((NG, 4, G, 64, HD), BF16),
            *[pltpu.VMEM((NY, G, 64, HD), BF16) for _ in range(2)],
            pltpu.VMEM((NG, NL, G, 16, HD), BF16),
            *[pltpu.VMEM((NL, G, 16, HD), BF16) for _ in range(2)],
            pltpu.VMEM((NG, G, 16, HD), BF16),
            *[pltpu.VMEM((NH, G, 16, HD), BF16) for _ in range(2)],
            pltpu.VMEM((NG, 16, G, 16, HD), BF16),
            pltpu.VMEM((HEADS, NT, TILE), F32),
            pltpu.VMEM((NT, TILE), F32),
            pltpu.VMEM((NY, NV, TILE), F32),
            pltpu.VMEM((NL * NH, NV, TILE), F32),
            dma((8,)), dma((2,)), dma((2,)),
            dma((NG * 15,)), dma((NG * 15,)), dma((18,)), dma((18,)), dma((8,)), dma((8,)),
        ],
        compiler_params=pltpu.CompilerParams(
            collective_id=0, has_side_effects=True, vmem_limit_bytes=56 << 20
        ),
    )(vertical_ids, slash_offsets, keep_counts, queries, keys.reshape(NT, TILE, HD), values.reshape(NT, TILE, HD))
    return attended, column.reshape(rows), vertical


def solution(mesh):
    placed = (
        P("ctx", "head"),
        P("ctx", "head"),
        P("ctx", "head"),
        P("head", None),
        P("head", None),
        P("head", "ctx"),
    )
    return jax.shard_map(
        local,
        mesh=mesh,
        in_specs=placed,
        out_specs=(P("ctx", "head"), P("ctx"), P("head", None, None)),
        check_vma=False,
    )
```

```python
import functools
import math

import jax
import jax.numpy as jnp
from jax import lax
from jax.experimental import pallas as pl
from jax.experimental.pallas import tpu as pltpu
from jax.sharding import PartitionSpec as P

MESH = pl.DeviceIdType.MESH
QPK = 4
TILE = 128
HD = 128
NV = 8
NT = 8
ROWS = QPK * TILE
NG = 2
G = NV // NG
NY = 4
NL = 4
NH = 4
HEADS = 8
CTX = NY * NL * NH
HIDE = -1e30
RATE = HD ** -0.5 * math.log2(math.e)
NEAR = (-1, -2, 1)
SLASH_K = 1
SLASH_V = 2
F32 = jnp.float32
BF16 = jnp.bfloat16


def dot_nt(a, b):
    return lax.dot_general(a, b, (((1,), (1,)), ((), ())), preferred_element_type=F32)


def kernel(vert_hbm, slash_hbm, keep_hbm, q_hbm, k_hbm, v_hbm, att, sums_ref,
           vert, slash, keep, q, ko, vo, kw, vw, kvert, vvert, causal, ebuf_a, ebuf_b, shares, mx, acc0, acc, sc, win, vs,
           s1, r1a, r1b, s2, r2a, r2b, s3, r3a, r3b, full,
           hr, rw, v1, vz,
           in_sem, slash_s, slash_r, ex_s, ex_r, far_s, far_r, t_s, t_r, h_s, h_r):
    head = lax.axis_index("head")
    ctx = lax.axis_index("ctx")
    y = ctx // (NL * NH)
    zh = (ctx // NL) % NH
    zl = ctx % NL
    z = ctx % (NL * NH)

    def at(a, b, c):
        return (head, a * (NL * NH) + b * NL + c)

    def along(k):
        return (head, y * (NL * NH) + (z + k + NL * NH) % (NL * NH))

    y_peers = [((y + k) % NY, at((y + k) % NY, zh, zl)) for k in (1, 2, 3)]
    h_peers = [((zh + k) % NH, at(y, (zh + k) % NH, zl)) for k in (2, 1, 3)]
    n_peers = [((zl + k + NL) % NL, along(k)) for k in NEAR]
    heads = [((head + k) % HEADS, ((head + k) % HEADS, ctx)) for k in range(1, HEADS)]
    after = (head, (ctx + 1) % CTX)
    before = (head, (ctx + CTX - 1) % CTX)

    barrier = pltpu.get_barrier_semaphore()
    z_peers = [along(k) for k in (8, 7, -7, 6, -6, 5, -5, 4, -4, 3, -3, 2, -2, 1, -1)]
    greeted = z_peers + [p for _, p in y_peers + heads] + [after, before]
    for p in greeted:
        pl.semaphore_signal(barrier, inc=1, device_id=p, device_id_type=MESH)

    loads = [
        pltpu.make_async_copy(k_hbm, ko, in_sem.at[0]),
        pltpu.make_async_copy(v_hbm, vo, in_sem.at[1]),
        pltpu.make_async_copy(q_hbm, q, in_sem.at[2]),
        pltpu.make_async_copy(k_hbm, kw.at[pl.ds(NT, NT)], in_sem.at[3]),
        pltpu.make_async_copy(v_hbm, vw.at[pl.ds(NT, NT)], in_sem.at[4]),
    ]
    small = [
        pltpu.make_async_copy(vert_hbm, vert, in_sem.at[5]),
        pltpu.make_async_copy(slash_hbm, slash, in_sem.at[6]),
        pltpu.make_async_copy(keep_hbm, keep, in_sem.at[7]),
    ]
    for c in small + loads:
        c.start()

    def remote(src, dst, ss, rs, p):
        return pltpu.make_async_remote_copy(
            src_ref=src, dst_ref=dst, send_sem=ss, recv_sem=rs, device_id=p, device_id_type=MESH
        )

    row = lax.broadcasted_iota(jnp.int32, (ROWS, HD), 0) % TILE
    lane = lax.broadcasted_iota(jnp.int32, (ROWS, HD), 1)
    causal[...] = jnp.where((lane == 0) | (lane > row), 1.0, 0.0).astype(BF16)

    for c in small + loads[:2]:
        c.wait()
    for j in range(NV):
        g, jj = divmod(j, G)
        for part, ref in ((0, ko), (1, vo)):
            tile = ref[vert[0, j] & (NT - 1)]
            for piece in range(8):
                of_y, of_l = divmod(8 * part + piece, NL)
                rows = tile[16 * piece:16 * piece + 16]
                if g == 0:
                    s1[g, of_y, jj, 16 * of_l:16 * of_l + 16] = rows
                else:
                    s1[g, of_l, jj, 16 * of_y:16 * of_y + 16] = rows
    r1 = (r1a, r1b)
    r2 = (r2a, r2b)
    r3 = (r3a, r3b)
    mine = ((y, zl), (zl, y))
    peers = ((y_peers, n_peers), (n_peers, y_peers))
    for g in range(NG):
        r1[g][mine[g][0]] = s1[g, mine[g][0]]

    pl.semaphore_wait(barrier, len(greeted))

    def stage(g, number, peers, src, dst):
        base = (g * 5 + number) * 3
        return [
            remote(src(i), dst(i), ex_s.at[base + n], ex_r.at[base + n], p)
            for n, (i, p) in enumerate(peers)
        ]

    steps = {}
    for g in range(NG):
        if g == 0:
            steps[g, 0] = stage(g, 0, peers[g][0], lambda i: s1.at[g, i], lambda i: r1[g].at[mine[g][0]])
        else:
            split = [(zl + NL - 1) % NL, (zl + 1) % NL] + [(zl + 2) % NL] * 2
            slots = [pl.ds(0, G)] * 2 + [pl.ds(0, G // 2), pl.ds(G // 2, G // 2)]
            steps[g, 0] = [
                remote(s1.at[g, i, part], r1[g].at[zl, part], far_s.at[n], far_r.at[n], along(k))
                for n, (i, part, k) in enumerate(zip(split, slots, (-1, 1, -2, 2)))
            ]
        for c in steps[g, 0]:
            c.start()
    lower = pl.ds(0, NT)
    slash_copies = [
        remote(ko, kw.at[lower], slash_s.at[0], slash_r.at[0], after),
        remote(vo, vw.at[lower], slash_s.at[1], slash_r.at[1], after),
    ]

    def send_slash(number):
        for c, when in zip(slash_copies, (SLASH_K, SLASH_V)):
            if when == number:
                c.start()

    send_slash(0)

    def owner(j, low, count):
        return (vert[0, j] >> low) & (count - 1)

    def arrived(g, number):
        for c in steps[g, number]:
            c.wait_recv()

    for g in range(NG):
        arrived(g, 0)
        for jj in range(G):
            j = g * G + jj
            src = owner(j, 7, NY) if g == 0 else owner(j, 3, NL)
            block = r1[g][src, jj]
            for n in range(4):
                s2[g, n, jj] = block[16 * n:16 * n + 16]
        r2[g][mine[g][1]] = s2[g, mine[g][1]]
        steps[g, 1] = stage(g, 1, peers[g][1], lambda i: s2.at[g, i], lambda i: r2[g].at[mine[g][1]])
        for c in steps[g, 1]:
            c.start()
    send_slash(1)
    for g in range(NG):
        arrived(g, 1)
        for jj in range(G):
            j = g * G + jj
            src = owner(j, 3, NL) if g == 0 else owner(j, 7, NY)
            s3[g, jj] = r2[g][src, jj]
        r3[g][zh] = s3[g]
        steps[g, 2] = stage(g, 2, h_peers, lambda i: s3.at[g], lambda i: r3[g].at[zh])
        for c in steps[g, 2]:
            c.start()
    send_slash(2)

    piece = (4 * y + zl, 4 * zl + y)
    for g in range(NG):
        arrived(g, 2)
        for jj in range(G):
            j = g * G + jj
            low = 1 if g == 1 and jj >= G // 2 else 2
            of = owner(j, 3, NL * NH)
            gathered = (of + ((zl - of + low) & (NL - 1)) - low) & (NL * NH - 1)
            full[g, piece[g], jj] = r3[g][gathered >> 2, jj]
        steps[g, 3] = stage(g, 3, peers[g][1], lambda i: full.at[g, piece[g]], lambda i: full.at[g, piece[g]])
        for c in steps[g, 3]:
            c.start()
    send_slash(3)
    for g in range(NG):
        arrived(g, 3)
        block = pl.ds(4 * mine[g][0], 4)
        steps[g, 4] = stage(g, 4, peers[g][0], lambda i: full.at[g, block], lambda i: full.at[g, block])
        for c in steps[g, 4]:
            c.start()
    send_slash(4)

    for c in loads[2:]:
        c.wait()
    slash_copies[0].wait_recv()
    key_row = lax.broadcasted_iota(jnp.int32, (TILE, HD), 0)
    key_lane = lax.broadcasted_iota(jnp.int32, (TILE, HD), 1)
    near = slash[0, 1]

    def stacked(i):
        rows = q[pl.ds(pl.multiple_of(i * TILE, TILE), TILE), :]
        return jnp.concatenate([rows[:, h * HD:(h + 1) * HD] for h in range(QPK)], axis=0)

    def soft(scores):
        top = jnp.max(scores, axis=1, keepdims=True)
        return top, jnp.exp2((scores - top) * RATE).astype(BF16)

    def mixed(weights, value_rows):
        ones = jnp.ones(value_rows.shape, BF16)
        return jnp.dot(weights, jnp.concatenate([value_rows, ones], axis=1), preferred_element_type=F32)

    def first(i, _):
        t = ctx * NT + i
        keys = jnp.concatenate([kw[NT + i], kw[i], kw[NT + i - near]], axis=0)
        diagonal = jnp.where((key_row == key_lane) & (key_lane > 0), HIDE, 0.0).astype(BF16)
        far_bias = jnp.where((key_lane == 0) & (key_lane + t < slash[0, 0]), HIDE, 0.0).astype(BF16)
        near_bias = jnp.where((key_lane == 0) & (key_lane + t < near), HIDE, 0.0).astype(BF16)
        bias = jnp.concatenate([diagonal, far_bias, near_bias], axis=0)
        query = jnp.concatenate([stacked(i), causal[...]], axis=1)
        scores = dot_nt(query, jnp.concatenate([keys, bias], axis=1))
        top, weights = soft(scores)
        ebuf_a[i] = weights
        mx[0, i] = jnp.broadcast_to(top, (ROWS, HD))
        return 0

    lax.fori_loop(0, NT, first, 0, unroll=4)

    slash_copies[1].wait_recv()

    def mix(i, _):
        values = jnp.concatenate([vw[NT + i], vw[i], vw[NT + i - near]], axis=0)
        acc0[i] = mixed(ebuf_a[i], values)
        return 0

    lax.fori_loop(0, NT, mix, 0, unroll=4)

    lanes8 = lax.broadcasted_iota(jnp.int32, (8, HD), 1)
    ids = jnp.zeros((8, HD), jnp.int32)
    for j in range(NV):
        ids = jnp.where(lanes8 == j, vert[0, j], ids)
    slot_row = lax.broadcasted_iota(jnp.int32, (G * TILE, HD), 0) // TILE
    slot_lane = lax.broadcasted_iota(jnp.int32, (G * TILE, HD), 1)

    def flags(i):
        t = ctx * NT + i
        valid = (lanes8 < keep[0, i]) & (ids < t) & (ids != t - slash[0, 0]) & (ids != t - near)
        flag = jnp.where(valid | (lanes8 >= NV), 0.0, 1.0)
        return jnp.broadcast_to(flag[:1], (ROWS, HD)).astype(BF16)

    for g in range(NG):
        arrived(g, 4)
        for jj in range(G):
            order = [p if g == 0 else 4 * (p % 4) + p // 4 for p in range(16)]
            kvert[g, jj] = jnp.concatenate([full[g, p, jj] for p in order[:8]], axis=0)
            vvert[g, jj] = jnp.concatenate([full[g, p, jj] for p in order[8:]], axis=0)
        bias = jnp.where(slot_row + g * G == slot_lane, HIDE, 0.0).astype(BF16)

        def vertical(i, _):
            keys = kvert[g].reshape(G * TILE, HD)
            values = vvert[g].reshape(G * TILE, HD)
            query = jnp.concatenate([stacked(i), flags(i)], axis=1)
            scores = dot_nt(query, jnp.concatenate([keys, bias], axis=1))
            top, weights = soft(scores)
            ebuf_b[g, i] = weights
            mx[g + 1, i] = jnp.broadcast_to(top, (ROWS, HD))
            acc[g, i] = mixed(weights, values)
            return 0

        lax.fori_loop(0, NT, vertical, 0, unroll=8)

    lane_id = lax.broadcasted_iota(jnp.int32, (ROWS, HD), 1)
    win_row = lax.broadcasted_iota(jnp.int32, (2 * NT, TILE), 0)
    vs_row = lax.broadcasted_iota(jnp.int32, (NV, TILE), 0)

    def sums(rows, weights, which):
        both = jnp.dot(rows, weights, preferred_element_type=F32)
        return both[which:which + 1] + both[8 + which:9 + which]

    def finish(i, vertical_sums):
        tops = [mx[x, i] for x in range(NG + 1)]
        top = functools.reduce(jnp.maximum, tops)
        scales = [jnp.exp2((t - top) * RATE) for t in tops]
        total = acc0[i, :, HD:] * scales[0]
        for g in range(NG):
            total = total + acc[g, i, :, HD:] * scales[g + 1]
        inverse = 1.0 / total
        scales = [f * inverse for f in scales]
        for x in range(NG + 1):
            sc[x, i] = scales[x]
        factors = scales[0]
        for x in range(1, NG + 1):
            factors = jnp.where(lane_id == x, scales[x], factors)
        turned = jnp.transpose(factors)[:8]
        high = turned.astype(BF16)
        low = (turned - high.astype(F32)).astype(BF16)
        rows = jnp.concatenate([high, low], axis=0)
        shares[i] = rows

        for g in range(NG):
            part = sums(rows, ebuf_b[g, i], g + 1)
            for jj in range(G):
                here = vs_row == g * G + jj
                vertical_sums = vertical_sums + jnp.where(here, part[:, jj * TILE:(jj + 1) * TILE], 0.0)
        return vertical_sums

    vs[...] = lax.fori_loop(0, NT, finish, jnp.zeros((NV, TILE), F32), unroll=8)

    v1[y] = vs[...]
    c1 = [remote(vs, v1.at[y], t_s.at[n], t_r.at[n], p) for n, (_, p) in enumerate(y_peers)]
    for c in c1:
        c.start()

    def near_sums(i, window_sums):
        part = sums(shares[i], ebuf_a[i], 0)
        add = jnp.where(win_row == NT + i, part[:, :TILE], 0.0)
        add = add + jnp.where(win_row == i, part[:, TILE:2 * TILE], 0.0)
        add = add + jnp.where(win_row == NT + i - near, part[:, 2 * TILE:], 0.0)
        return window_sums + add

    win[...] = lax.fori_loop(0, NT, near_sums, jnp.zeros((2 * NT, TILE), F32), unroll=4)
    to_before = remote(win.at[pl.ds(0, NT)], rw, h_s.at[7], h_r.at[7], before)
    to_before.start()
    for c in c1:
        c.wait_recv()
    vz[z] = (v1[0] + v1[1]) + (v1[2] + v1[3])
    c2 = [remote(vz.at[z], vz.at[z], t_s.at[3 + n], t_r.at[3 + n], p) for n, p in enumerate(z_peers)]
    for c in c2:
        c.start()

    def normalise(i, _):
        out = acc0[i, :, :HD] * sc[0, i]
        for g in range(NG):
            out = out + acc[g, i, :, :HD] * sc[g + 1, i]
        out = out.astype(BF16)
        here = pl.ds(pl.multiple_of(i * TILE, TILE), TILE)
        att[here, :] = jnp.concatenate([out[h * TILE:(h + 1) * TILE] for h in range(QPK)], axis=1)
        return 0

    lax.fori_loop(0, NT // 2, normalise, 0)
    to_before.wait_recv()
    hr[head] = win[NT:] + rw[...]
    ch = [remote(hr.at[head], hr.at[head], h_s.at[n], h_r.at[n], p) for n, (_, p) in enumerate(heads)]
    for c in ch:
        c.start()
    lax.fori_loop(NT // 2, NT, normalise, 0)
    for c in ch:
        c.wait_recv()
    total = hr[0]
    for n in range(1, HEADS):
        total = total + hr[n]
    sums_ref[0] = total * (1.0 / (HEADS * QPK))
    for c in [c for group in steps.values() for c in group] + slash_copies + [to_before] + c1:
        c.wait_send()
    for c in c2:
        c.wait_recv()
    total = vz[0]
    for n in range(1, NL * NH):
        total = total + vz[n]
    sums_ref[1] = total * (1.0 / QPK)

    for c in c2 + ch:
        c.wait_send()


def local(queries, keys, values, vertical_ids, slash_offsets, keep_counts):
    rows = keys.shape[0]
    vmem = pl.BlockSpec(memory_space=pltpu.VMEM)
    hbm = pl.BlockSpec(memory_space=pl.ANY)
    dma = pltpu.SemaphoreType.DMA
    attended, both = pl.pallas_call(
        kernel,
        out_shape=(
            pltpu.VMEM(queries.shape, BF16),
            pltpu.VMEM((2, NT, TILE), F32),
        ),
        in_specs=[hbm] * 6,
        out_specs=(vmem, vmem),
        scratch_shapes=[
            *[pltpu.SMEM(a.shape, jnp.int32) for a in (vertical_ids, slash_offsets, keep_counts)],
            pltpu.VMEM((rows, QPK * HD), BF16),
            *[pltpu.VMEM((NT, TILE, HD), BF16) for _ in range(2)],
            *[pltpu.VMEM((2 * NT, TILE, HD), BF16) for _ in range(2)],
            *[pltpu.VMEM((NG, G, TILE, HD), BF16) for _ in range(2)],
            pltpu.VMEM((ROWS, HD), BF16),
            pltpu.VMEM((NT, ROWS, 3 * TILE), BF16),
            pltpu.VMEM((NG, NT, ROWS, G * TILE), BF16),
            pltpu.VMEM((NT, 16, ROWS), BF16),
            pltpu.VMEM((NG + 1, NT, ROWS, HD), F32),
            pltpu.VMEM((NT, ROWS, 2 * HD), F32),
            pltpu.VMEM((NG, NT, ROWS, 2 * HD), F32),
            pltpu.VMEM((NG + 1, NT, ROWS, HD), F32),
            pltpu.VMEM((2 * NT, TILE), F32),
            pltpu.VMEM((NV, TILE), F32),
            pltpu.VMEM((NG, 4, G, 64, HD), BF16),
            *[pltpu.VMEM((NY, G, 64, HD), BF16) for _ in range(2)],
            pltpu.VMEM((NG, NL, G, 16, HD), BF16),
            *[pltpu.VMEM((NL, G, 16, HD), BF16) for _ in range(2)],
            pltpu.VMEM((NG, G, 16, HD), BF16),
            *[pltpu.VMEM((NH, G, 16, HD), BF16) for _ in range(2)],
            pltpu.VMEM((NG, 16, G, 16, HD), BF16),
            pltpu.VMEM((HEADS, NT, TILE), F32),
            pltpu.VMEM((NT, TILE), F32),
            pltpu.VMEM((NY, NV, TILE), F32),
            pltpu.VMEM((NL * NH, NV, TILE), F32),
            dma((8,)), dma((2,)), dma((2,)),
            dma((NG * 15,)), dma((NG * 15,)), dma((4,)), dma((4,)), dma((18,)), dma((18,)), dma((8,)), dma((8,)),
        ],
        compiler_params=pltpu.CompilerParams(
            collective_id=0, has_side_effects=True, vmem_limit_bytes=56 << 20
        ),
    )(vertical_ids, slash_offsets, keep_counts, queries, keys.reshape(NT, TILE, HD), values.reshape(NT, TILE, HD))
    return attended, both[0].reshape(rows), both[1:]


def solution(mesh):
    placed = (
        P("ctx", "head"),
        P("ctx", "head"),
        P("ctx", "head"),
        P("head", None),
        P("head", None),
        P("head", "ctx"),
    )
    return jax.shard_map(
        local,
        mesh=mesh,
        in_specs=placed,
        out_specs=(P("ctx", "head"), P("ctx"), P("head", None, None)),
        check_vma=False,
    )
```

```python
import functools
import math

import jax
import jax.numpy as jnp
from jax import lax
from jax.experimental import pallas as pl
from jax.experimental.pallas import tpu as pltpu
from jax.sharding import PartitionSpec as P

MESH = pl.DeviceIdType.MESH
QPK = 4
TILE = 128
HD = 128
NV = 8
NT = 8
ROWS = QPK * TILE
NG = 2
G = NV // NG
NY = 4
NL = 4
NH = 4
HEADS = 8
CTX = NY * NL * NH
HIDE = -1e30
RATE = HD ** -0.5 * math.log2(math.e)
NEAR = (-1, -2, 1)
SLASH_K = 1
SLASH_V = 2
F32 = jnp.float32
BF16 = jnp.bfloat16


def dot_nt(a, b):
    return lax.dot_general(a, b, (((1,), (1,)), ((), ())), preferred_element_type=F32)


def kernel(vert_hbm, slash_hbm, keep_hbm, q_hbm, k_hbm, v_hbm, att, sums_ref,
           vert, slash, keep, q, ko, vo, kw, vw, kvert, vvert, causal, ebuf_a, ebuf_b, shares, mx, acc0, acc, sc, win, vs,
           s1, r1a, r1b, s2, r2a, r2b, s3, r3a, r3b, full,
           hr, rw, v1, vz,
           in_sem, slash_s, slash_r, ex_s, ex_r, far_s, far_r, ready, t_s, t_r, h_s, h_r):
    head = lax.axis_index("head")
    ctx = lax.axis_index("ctx")
    y = ctx // (NL * NH)
    zh = (ctx // NL) % NH
    zl = ctx % NL
    z = ctx % (NL * NH)

    def at(a, b, c):
        return (head, a * (NL * NH) + b * NL + c)

    def along(k):
        return (head, y * (NL * NH) + (z + k + NL * NH) % (NL * NH))

    y_peers = [((y + k) % NY, at((y + k) % NY, zh, zl)) for k in (1, 2, 3)]
    h_peers = [((zh + k) % NH, at(y, (zh + k) % NH, zl)) for k in (2, 1, 3)]
    n_peers = [((zl + k + NL) % NL, along(k)) for k in NEAR]
    heads = [((head + k) % HEADS, ((head + k) % HEADS, ctx)) for k in range(1, HEADS)]
    after = (head, (ctx + 1) % CTX)
    before = (head, (ctx + CTX - 1) % CTX)

    barrier = pltpu.get_barrier_semaphore()
    z_peers = [along(k) for k in (8, 7, -7, 6, -6, 5, -5, 4, -4, 3, -3, 2, -2, 1, -1)]
    greeted = [along(k) for k in (2, -2, 1, -1)] + [p for _, p in y_peers + heads] + [after, before]
    for p in greeted:
        pl.semaphore_signal(barrier, inc=1, device_id=p, device_id_type=MESH)

    loads = [
        pltpu.make_async_copy(k_hbm, ko, in_sem.at[0]),
        pltpu.make_async_copy(v_hbm, vo, in_sem.at[1]),
        pltpu.make_async_copy(q_hbm, q, in_sem.at[2]),
        pltpu.make_async_copy(k_hbm, kw.at[pl.ds(NT, NT)], in_sem.at[3]),
        pltpu.make_async_copy(v_hbm, vw.at[pl.ds(NT, NT)], in_sem.at[4]),
    ]
    small = [
        pltpu.make_async_copy(vert_hbm, vert, in_sem.at[5]),
        pltpu.make_async_copy(slash_hbm, slash, in_sem.at[6]),
        pltpu.make_async_copy(keep_hbm, keep, in_sem.at[7]),
    ]
    for c in small + loads:
        c.start()

    def remote(src, dst, ss, rs, p):
        return pltpu.make_async_remote_copy(
            src_ref=src, dst_ref=dst, send_sem=ss, recv_sem=rs, device_id=p, device_id_type=MESH
        )

    row = lax.broadcasted_iota(jnp.int32, (ROWS, HD), 0) % TILE
    lane = lax.broadcasted_iota(jnp.int32, (ROWS, HD), 1)
    causal[...] = jnp.where((lane == 0) | (lane > row), 1.0, 0.0).astype(BF16)

    for c in small + loads[:2]:
        c.wait()
    for j in range(NV):
        g, jj = divmod(j, G)
        for part, ref in ((0, ko), (1, vo)):
            tile = ref[vert[0, j] & (NT - 1)]
            for piece in range(8):
                of_y, of_l = divmod(8 * part + piece, NL)
                rows = tile[16 * piece:16 * piece + 16]
                if g == 0:
                    s1[g, of_y, jj, 16 * of_l:16 * of_l + 16] = rows
                else:
                    s1[g, of_l, jj, 16 * of_y:16 * of_y + 16] = rows
    r1 = (r1a, r1b)
    r2 = (r2a, r2b)
    r3 = (r3a, r3b)
    mine = ((y, zl), (zl, y))
    peers = ((y_peers, n_peers), (n_peers, y_peers))
    for g in range(NG):
        r1[g][mine[g][0]] = s1[g, mine[g][0]]

    pl.semaphore_wait(barrier, len(greeted))

    def stage(g, number, peers, src, dst):
        base = (g * 5 + number) * 3
        return [
            remote(src(i), dst(i), ex_s.at[base + n], ex_r.at[base + n], p)
            for n, (i, p) in enumerate(peers)
        ]

    steps = {}
    for g in range(NG):
        if g == 0:
            steps[g, 0] = stage(g, 0, peers[g][0], lambda i: s1.at[g, i], lambda i: r1[g].at[mine[g][0]])
        else:
            split = [(zl + NL - 1) % NL, (zl + 1) % NL] + [(zl + 2) % NL] * 2
            slots = [pl.ds(0, G)] * 2 + [pl.ds(0, G // 2), pl.ds(G // 2, G // 2)]
            steps[g, 0] = [
                remote(s1.at[g, i, part], r1[g].at[zl, part], far_s.at[n], far_r.at[n], along(k))
                for n, (i, part, k) in enumerate(zip(split, slots, (-1, 1, -2, 2)))
            ]
        for c in steps[g, 0]:
            c.start()
    lower = pl.ds(0, NT)
    slash_copies = [
        remote(ko, kw.at[lower], slash_s.at[0], slash_r.at[0], after),
        remote(vo, vw.at[lower], slash_s.at[1], slash_r.at[1], after),
    ]

    def send_slash(number):
        for c, when in zip(slash_copies, (SLASH_K, SLASH_V)):
            if when == number:
                c.start()

    send_slash(0)

    def tell(first, distance):
        for n, k in enumerate((distance, -distance)):
            pl.semaphore_signal(ready.at[first + n], inc=1, device_id=along(k), device_id_type=MESH)

    def told(first):
        for n in range(2):
            pl.semaphore_wait(ready.at[first + n], 1)

    tell(0, 2)
    told(0)
    tell(2, 4)

    def owner(j, low, count):
        return (vert[0, j] >> low) & (count - 1)

    def arrived(g, number):
        for c in steps[g, number]:
            c.wait_recv()

    for g in range(NG):
        arrived(g, 0)
        for jj in range(G):
            j = g * G + jj
            src = owner(j, 7, NY) if g == 0 else owner(j, 3, NL)
            block = r1[g][src, jj]
            for n in range(4):
                s2[g, n, jj] = block[16 * n:16 * n + 16]
        r2[g][mine[g][1]] = s2[g, mine[g][1]]
        steps[g, 1] = stage(g, 1, peers[g][1], lambda i: s2.at[g, i], lambda i: r2[g].at[mine[g][1]])
        for c in steps[g, 1]:
            c.start()
    send_slash(1)
    told(2)
    for g in range(NG):
        arrived(g, 1)
        for jj in range(G):
            j = g * G + jj
            src = owner(j, 3, NL) if g == 0 else owner(j, 7, NY)
            s3[g, jj] = r2[g][src, jj]
        r3[g][zh] = s3[g]
        steps[g, 2] = stage(g, 2, h_peers, lambda i: s3.at[g], lambda i: r3[g].at[zh])
        for c in steps[g, 2]:
            c.start()
    send_slash(2)

    piece = (4 * y + zl, 4 * zl + y)
    for g in range(NG):
        arrived(g, 2)
        for jj in range(G):
            j = g * G + jj
            low = 1 if g == 1 and jj >= G // 2 else 2
            of = owner(j, 3, NL * NH)
            gathered = (of + ((zl - of + low) & (NL - 1)) - low) & (NL * NH - 1)
            full[g, piece[g], jj] = r3[g][gathered >> 2, jj]
        steps[g, 3] = stage(g, 3, peers[g][1], lambda i: full.at[g, piece[g]], lambda i: full.at[g, piece[g]])
        for c in steps[g, 3]:
            c.start()
    send_slash(3)
    for g in range(NG):
        arrived(g, 3)
        block = pl.ds(4 * mine[g][0], 4)
        steps[g, 4] = stage(g, 4, peers[g][0], lambda i: full.at[g, block], lambda i: full.at[g, block])
        for c in steps[g, 4]:
            c.start()
    send_slash(4)

    for c in loads[2:]:
        c.wait()
    slash_copies[0].wait_recv()
    key_row = lax.broadcasted_iota(jnp.int32, (TILE, HD), 0)
    key_lane = lax.broadcasted_iota(jnp.int32, (TILE, HD), 1)
    near = slash[0, 1]

    def stacked(i):
        rows = q[pl.ds(pl.multiple_of(i * TILE, TILE), TILE), :]
        return jnp.concatenate([rows[:, h * HD:(h + 1) * HD] for h in range(QPK)], axis=0)

    def soft(scores):
        top = jnp.max(scores, axis=1, keepdims=True)
        return top, jnp.exp2((scores - top) * RATE).astype(BF16)

    def mixed(weights, value_rows):
        ones = jnp.ones(value_rows.shape, BF16)
        return jnp.dot(weights, jnp.concatenate([value_rows, ones], axis=1), preferred_element_type=F32)

    def first(i, _):
        t = ctx * NT + i
        keys = jnp.concatenate([kw[NT + i], kw[i], kw[NT + i - near]], axis=0)
        diagonal = jnp.where((key_row == key_lane) & (key_lane > 0), HIDE, 0.0).astype(BF16)
        far_bias = jnp.where((key_lane == 0) & (key_lane + t < slash[0, 0]), HIDE, 0.0).astype(BF16)
        near_bias = jnp.where((key_lane == 0) & (key_lane + t < near), HIDE, 0.0).astype(BF16)
        bias = jnp.concatenate([diagonal, far_bias, near_bias], axis=0)
        query = jnp.concatenate([stacked(i), causal[...]], axis=1)
        scores = dot_nt(query, jnp.concatenate([keys, bias], axis=1))
        top, weights = soft(scores)
        ebuf_a[i] = weights
        mx[0, i] = jnp.broadcast_to(top, (ROWS, HD))
        return 0

    lax.fori_loop(0, NT, first, 0, unroll=4)

    slash_copies[1].wait_recv()

    def mix(i, _):
        values = jnp.concatenate([vw[NT + i], vw[i], vw[NT + i - near]], axis=0)
        acc0[i] = mixed(ebuf_a[i], values)
        return 0

    lax.fori_loop(0, NT, mix, 0, unroll=4)

    lanes8 = lax.broadcasted_iota(jnp.int32, (8, HD), 1)
    ids = jnp.zeros((8, HD), jnp.int32)
    for j in range(NV):
        ids = jnp.where(lanes8 == j, vert[0, j], ids)
    slot_row = lax.broadcasted_iota(jnp.int32, (G * TILE, HD), 0) // TILE
    slot_lane = lax.broadcasted_iota(jnp.int32, (G * TILE, HD), 1)

    def flags(i):
        t = ctx * NT + i
        valid = (lanes8 < keep[0, i]) & (ids < t) & (ids != t - slash[0, 0]) & (ids != t - near)
        flag = jnp.where(valid | (lanes8 >= NV), 0.0, 1.0)
        return jnp.broadcast_to(flag[:1], (ROWS, HD)).astype(BF16)

    for g in range(NG):
        arrived(g, 4)
        for jj in range(G):
            order = [p if g == 0 else 4 * (p % 4) + p // 4 for p in range(16)]
            kvert[g, jj] = jnp.concatenate([full[g, p, jj] for p in order[:8]], axis=0)
            vvert[g, jj] = jnp.concatenate([full[g, p, jj] for p in order[8:]], axis=0)
        bias = jnp.where(slot_row + g * G == slot_lane, HIDE, 0.0).astype(BF16)

        def vertical(i, _):
            keys = kvert[g].reshape(G * TILE, HD)
            values = vvert[g].reshape(G * TILE, HD)
            query = jnp.concatenate([stacked(i), flags(i)], axis=1)
            scores = dot_nt(query, jnp.concatenate([keys, bias], axis=1))
            top, weights = soft(scores)
            ebuf_b[g, i] = weights
            mx[g + 1, i] = jnp.broadcast_to(top, (ROWS, HD))
            acc[g, i] = mixed(weights, values)
            return 0

        lax.fori_loop(0, NT, vertical, 0, unroll=8)

    lane_id = lax.broadcasted_iota(jnp.int32, (ROWS, HD), 1)
    win_row = lax.broadcasted_iota(jnp.int32, (2 * NT, TILE), 0)
    vs_row = lax.broadcasted_iota(jnp.int32, (NV, TILE), 0)

    def sums(rows, weights, which):
        both = jnp.dot(rows, weights, preferred_element_type=F32)
        return both[which:which + 1] + both[8 + which:9 + which]

    def finish(i, vertical_sums):
        tops = [mx[x, i] for x in range(NG + 1)]
        top = functools.reduce(jnp.maximum, tops)
        scales = [jnp.exp2((t - top) * RATE) for t in tops]
        total = acc0[i, :, HD:] * scales[0]
        for g in range(NG):
            total = total + acc[g, i, :, HD:] * scales[g + 1]
        inverse = 1.0 / total
        scales = [f * inverse for f in scales]
        for x in range(NG + 1):
            sc[x, i] = scales[x]
        factors = scales[0]
        for x in range(1, NG + 1):
            factors = jnp.where(lane_id == x, scales[x], factors)
        turned = jnp.transpose(factors)[:8]
        high = turned.astype(BF16)
        low = (turned - high.astype(F32)).astype(BF16)
        rows = jnp.concatenate([high, low], axis=0)
        shares[i] = rows

        for g in range(NG):
            part = sums(rows, ebuf_b[g, i], g + 1)
            for jj in range(G):
                here = vs_row == g * G + jj
                vertical_sums = vertical_sums + jnp.where(here, part[:, jj * TILE:(jj + 1) * TILE], 0.0)
        return vertical_sums

    vs[...] = lax.fori_loop(0, NT, finish, jnp.zeros((NV, TILE), F32), unroll=8)

    v1[y] = vs[...]
    c1 = [remote(vs, v1.at[y], t_s.at[n], t_r.at[n], p) for n, (_, p) in enumerate(y_peers)]
    for c in c1:
        c.start()

    def near_sums(i, window_sums):
        part = sums(shares[i], ebuf_a[i], 0)
        add = jnp.where(win_row == NT + i, part[:, :TILE], 0.0)
        add = add + jnp.where(win_row == i, part[:, TILE:2 * TILE], 0.0)
        add = add + jnp.where(win_row == NT + i - near, part[:, 2 * TILE:], 0.0)
        return window_sums + add

    win[...] = lax.fori_loop(0, NT, near_sums, jnp.zeros((2 * NT, TILE), F32), unroll=4)
    to_before = remote(win.at[pl.ds(0, NT)], rw, h_s.at[7], h_r.at[7], before)
    to_before.start()
    for c in c1:
        c.wait_recv()
    vz[z] = (v1[0] + v1[1]) + (v1[2] + v1[3])
    c2 = [remote(vz.at[z], vz.at[z], t_s.at[3 + n], t_r.at[3 + n], p) for n, p in enumerate(z_peers)]
    for c in c2:
        c.start()

    def normalise(i, _):
        out = acc0[i, :, :HD] * sc[0, i]
        for g in range(NG):
            out = out + acc[g, i, :, :HD] * sc[g + 1, i]
        out = out.astype(BF16)
        here = pl.ds(pl.multiple_of(i * TILE, TILE), TILE)
        att[here, :] = jnp.concatenate([out[h * TILE:(h + 1) * TILE] for h in range(QPK)], axis=1)
        return 0

    lax.fori_loop(0, NT // 2, normalise, 0)
    to_before.wait_recv()
    hr[head] = win[NT:] + rw[...]
    ch = [remote(hr.at[head], hr.at[head], h_s.at[n], h_r.at[n], p) for n, (_, p) in enumerate(heads)]
    for c in ch:
        c.start()
    lax.fori_loop(NT // 2, NT, normalise, 0)
    for c in ch:
        c.wait_recv()
    total = hr[0]
    for n in range(1, HEADS):
        total = total + hr[n]
    sums_ref[0] = total * (1.0 / (HEADS * QPK))
    for c in [c for group in steps.values() for c in group] + slash_copies + [to_before] + c1:
        c.wait_send()
    for c in c2:
        c.wait_recv()
    total = vz[0]
    for n in range(1, NL * NH):
        total = total + vz[n]
    sums_ref[1] = total * (1.0 / QPK)

    for c in c2 + ch:
        c.wait_send()


def local(queries, keys, values, vertical_ids, slash_offsets, keep_counts):
    rows = keys.shape[0]
    vmem = pl.BlockSpec(memory_space=pltpu.VMEM)
    hbm = pl.BlockSpec(memory_space=pl.ANY)
    dma = pltpu.SemaphoreType.DMA
    attended, both = pl.pallas_call(
        kernel,
        out_shape=(
            pltpu.VMEM(queries.shape, BF16),
            pltpu.VMEM((2, NT, TILE), F32),
        ),
        in_specs=[hbm] * 6,
        out_specs=(vmem, vmem),
        scratch_shapes=[
            *[pltpu.SMEM(a.shape, jnp.int32) for a in (vertical_ids, slash_offsets, keep_counts)],
            pltpu.VMEM((rows, QPK * HD), BF16),
            *[pltpu.VMEM((NT, TILE, HD), BF16) for _ in range(2)],
            *[pltpu.VMEM((2 * NT, TILE, HD), BF16) for _ in range(2)],
            *[pltpu.VMEM((NG, G, TILE, HD), BF16) for _ in range(2)],
            pltpu.VMEM((ROWS, HD), BF16),
            pltpu.VMEM((NT, ROWS, 3 * TILE), BF16),
            pltpu.VMEM((NG, NT, ROWS, G * TILE), BF16),
            pltpu.VMEM((NT, 16, ROWS), BF16),
            pltpu.VMEM((NG + 1, NT, ROWS, HD), F32),
            pltpu.VMEM((NT, ROWS, 2 * HD), F32),
            pltpu.VMEM((NG, NT, ROWS, 2 * HD), F32),
            pltpu.VMEM((NG + 1, NT, ROWS, HD), F32),
            pltpu.VMEM((2 * NT, TILE), F32),
            pltpu.VMEM((NV, TILE), F32),
            pltpu.VMEM((NG, 4, G, 64, HD), BF16),
            *[pltpu.VMEM((NY, G, 64, HD), BF16) for _ in range(2)],
            pltpu.VMEM((NG, NL, G, 16, HD), BF16),
            *[pltpu.VMEM((NL, G, 16, HD), BF16) for _ in range(2)],
            pltpu.VMEM((NG, G, 16, HD), BF16),
            *[pltpu.VMEM((NH, G, 16, HD), BF16) for _ in range(2)],
            pltpu.VMEM((NG, 16, G, 16, HD), BF16),
            pltpu.VMEM((HEADS, NT, TILE), F32),
            pltpu.VMEM((NT, TILE), F32),
            pltpu.VMEM((NY, NV, TILE), F32),
            pltpu.VMEM((NL * NH, NV, TILE), F32),
            dma((8,)), dma((2,)), dma((2,)),
            dma((NG * 15,)), dma((NG * 15,)), dma((4,)), dma((4,)), pltpu.SemaphoreType.REGULAR((4,)), dma((18,)), dma((18,)), dma((8,)), dma((8,)),
        ],
        compiler_params=pltpu.CompilerParams(
            collective_id=0, has_side_effects=True, vmem_limit_bytes=56 << 20
        ),
    )(vertical_ids, slash_offsets, keep_counts, queries, keys.reshape(NT, TILE, HD), values.reshape(NT, TILE, HD))
    return attended, both[0].reshape(rows), both[1:]


def solution(mesh):
    placed = (
        P("ctx", "head"),
        P("ctx", "head"),
        P("ctx", "head"),
        P("head", None),
        P("head", None),
        P("head", "ctx"),
    )
    return jax.shard_map(
        local,
        mesh=mesh,
        in_specs=placed,
        out_specs=(P("ctx", "head"), P("ctx"), P("head", None, None)),
        check_vma=False,
    )
```

```python
import functools
import math

import jax
import jax.numpy as jnp
from jax import lax
from jax.experimental import pallas as pl
from jax.experimental.pallas import tpu as pltpu
from jax.sharding import PartitionSpec as P

MESH = pl.DeviceIdType.MESH
QPK = 4
TILE = 128
HD = 128
NV = 8
NT = 8
ROWS = QPK * TILE
NG = 2
G = NV // NG
NY = 4
NL = 4
NH = 4
HEADS = 8
CTX = NY * NL * NH
HIDE = -1e30
RATE = HD ** -0.5 * math.log2(math.e)
NEAR = (-1, -2, 1)
SLASH_K = 1
SLASH_V = 2
F32 = jnp.float32
BF16 = jnp.bfloat16


def dot_nt(a, b):
    return lax.dot_general(a, b, (((1,), (1,)), ((), ())), preferred_element_type=F32)


def kernel(vert_hbm, slash_hbm, keep_hbm, q_hbm, k_hbm, v_hbm, att, sums_ref,
           vert, slash, keep, q, ko, vo, kw, vw, kvert, vvert, causal, ebuf_a, ebuf_b, shares, mx, acc0, acc, sc, win, vs,
           s1, r1a, r1b, s2, r2a, r2b, s3, r3a, r3b, full,
           hr, rw, v1, vz,
           in_sem, slash_s, slash_r, ex_s, ex_r, far_s, far_r, last_s, last_r, ready, t_s, t_r, h_s, h_r):
    head = lax.axis_index("head")
    ctx = lax.axis_index("ctx")
    y = ctx // (NL * NH)
    zh = (ctx // NL) % NH
    zl = ctx % NL
    z = ctx % (NL * NH)

    def at(a, b, c):
        return (head, a * (NL * NH) + b * NL + c)

    def along(k):
        return (head, y * (NL * NH) + (z + k + NL * NH) % (NL * NH))

    y_peers = [((y + k) % NY, at((y + k) % NY, zh, zl)) for k in (1, 2, 3)]
    h_peers = [((zh + k) % NH, at(y, (zh + k) % NH, zl)) for k in (2, 1, 3)]
    n_peers = [((zl + k + NL) % NL, along(k)) for k in NEAR]
    heads = [((head + k) % HEADS, ((head + k) % HEADS, ctx)) for k in range(1, HEADS)]
    after = (head, (ctx + 1) % CTX)
    before = (head, (ctx + CTX - 1) % CTX)

    barrier = pltpu.get_barrier_semaphore()
    z_peers = [along(k) for k in (8, 7, -7, 6, -6, 5, -5, 4, -4, 3, -3, 2, -2, 1, -1)]
    greeted = [along(k) for k in (2, -2, 1, -1)] + [p for _, p in y_peers + heads] + [after, before]
    for p in greeted:
        pl.semaphore_signal(barrier, inc=1, device_id=p, device_id_type=MESH)

    loads = [
        pltpu.make_async_copy(k_hbm, ko, in_sem.at[0]),
        pltpu.make_async_copy(v_hbm, vo, in_sem.at[1]),
        pltpu.make_async_copy(q_hbm, q, in_sem.at[2]),
        pltpu.make_async_copy(k_hbm, kw.at[pl.ds(NT, NT)], in_sem.at[3]),
        pltpu.make_async_copy(v_hbm, vw.at[pl.ds(NT, NT)], in_sem.at[4]),
    ]
    small = [
        pltpu.make_async_copy(vert_hbm, vert, in_sem.at[5]),
        pltpu.make_async_copy(slash_hbm, slash, in_sem.at[6]),
        pltpu.make_async_copy(keep_hbm, keep, in_sem.at[7]),
    ]
    for c in small + loads:
        c.start()

    def remote(src, dst, ss, rs, p):
        return pltpu.make_async_remote_copy(
            src_ref=src, dst_ref=dst, send_sem=ss, recv_sem=rs, device_id=p, device_id_type=MESH
        )

    row = lax.broadcasted_iota(jnp.int32, (ROWS, HD), 0) % TILE
    lane = lax.broadcasted_iota(jnp.int32, (ROWS, HD), 1)
    causal[...] = jnp.where((lane == 0) | (lane > row), 1.0, 0.0).astype(BF16)

    for c in small + loads[:2]:
        c.wait()
    for j in range(NV):
        g, jj = divmod(j, G)
        for part, ref in ((0, ko), (1, vo)):
            tile = ref[vert[0, j] & (NT - 1)]
            for piece in range(8):
                of_y, of_l = divmod(8 * part + piece, NL)
                rows = tile[16 * piece:16 * piece + 16]
                if g == 0:
                    s1[g, of_y, jj, 16 * of_l:16 * of_l + 16] = rows
                else:
                    s1[g, of_l, jj, 16 * of_y:16 * of_y + 16] = rows
    r1 = (r1a, r1b)
    r2 = (r2a, r2b)
    r3 = (r3a, r3b)
    mine = ((y, zl), (zl, y))
    peers = ((y_peers, n_peers), (n_peers, y_peers))
    for g in range(NG):
        r1[g][mine[g][0]] = s1[g, mine[g][0]]

    pl.semaphore_wait(barrier, len(greeted))

    def stage(g, number, peers, src, dst):
        base = (g * 5 + number) * 3
        return [
            remote(src(i), dst(i), ex_s.at[base + n], ex_r.at[base + n], p)
            for n, (i, p) in enumerate(peers)
        ]

    steps = {}
    for g in range(NG):
        if g == 0:
            steps[g, 0] = stage(g, 0, peers[g][0], lambda i: s1.at[g, i], lambda i: r1[g].at[mine[g][0]])
        else:
            split = [(zl + NL - 1) % NL, (zl + 1) % NL] + [(zl + 2) % NL] * 2
            slots = [pl.ds(0, G)] * 2 + [pl.ds(0, G // 2), pl.ds(G // 2, G // 2)]
            steps[g, 0] = [
                remote(s1.at[g, i, part], r1[g].at[zl, part], far_s.at[n], far_r.at[n], along(k))
                for n, (i, part, k) in enumerate(zip(split, slots, (-1, 1, -2, 2)))
            ]
        for c in steps[g, 0]:
            c.start()
    lower = pl.ds(0, NT)
    slash_copies = [
        remote(ko, kw.at[lower], slash_s.at[0], slash_r.at[0], after),
        remote(vo, vw.at[lower], slash_s.at[1], slash_r.at[1], after),
    ]

    def send_slash(number):
        for c, when in zip(slash_copies, (SLASH_K, SLASH_V)):
            if when == number:
                c.start()

    send_slash(0)

    def tell(first, distance):
        for n, k in enumerate((distance, -distance)):
            pl.semaphore_signal(ready.at[first + n], inc=1, device_id=along(k), device_id_type=MESH)

    def told(first):
        for n in range(2):
            pl.semaphore_wait(ready.at[first + n], 1)

    tell(0, 2)
    told(0)
    tell(2, 4)

    def owner(j, low, count):
        return (vert[0, j] >> low) & (count - 1)

    def arrived(g, number):
        for c in steps[g, number]:
            c.wait_recv()

    for g in range(NG):
        arrived(g, 0)
        for jj in range(G):
            j = g * G + jj
            src = owner(j, 7, NY) if g == 0 else owner(j, 3, NL)
            block = r1[g][src, jj]
            for n in range(4):
                s2[g, n, jj] = block[16 * n:16 * n + 16]
        r2[g][mine[g][1]] = s2[g, mine[g][1]]
        steps[g, 1] = stage(g, 1, peers[g][1], lambda i: s2.at[g, i], lambda i: r2[g].at[mine[g][1]])
        for c in steps[g, 1]:
            c.start()
    send_slash(1)
    told(2)
    for g in range(NG):
        arrived(g, 1)
        for jj in range(G):
            j = g * G + jj
            src = owner(j, 3, NL) if g == 0 else owner(j, 7, NY)
            s3[g, jj] = r2[g][src, jj]
        r3[g][zh] = s3[g]
        steps[g, 2] = stage(g, 2, h_peers, lambda i: s3.at[g], lambda i: r3[g].at[zh])
        for c in steps[g, 2]:
            c.start()
    send_slash(2)

    piece = (4 * y + zl, 4 * zl + y)
    for g in range(NG):
        arrived(g, 2)
        for jj in range(G):
            j = g * G + jj
            low = 1 if g == 1 and jj >= G // 2 else 2
            of = owner(j, 3, NL * NH)
            gathered = (of + ((zl - of + low) & (NL - 1)) - low) & (NL * NH - 1)
            full[g, piece[g], jj] = r3[g][gathered >> 2, jj]
        steps[g, 3] = stage(g, 3, peers[g][1], lambda i: full.at[g, piece[g]], lambda i: full.at[g, piece[g]])
        for c in steps[g, 3]:
            c.start()
    send_slash(3)
    for g in range(NG):
        arrived(g, 3)
        block = pl.ds(4 * mine[g][0], 4)
        if g == 0:
            steps[g, 4] = stage(g, 4, y_peers, lambda i: full.at[g, block], lambda i: full.at[g, block])
        else:
            parts = [block] * 2 + [pl.ds(4 * zl, 2), pl.ds(4 * zl + 2, 2)]
            steps[g, 4] = [
                remote(full.at[g, part], full.at[g, part], last_s.at[n], last_r.at[n], along(k))
                for n, (part, k) in enumerate(zip(parts, (-1, 1, -2, 2)))
            ]
        for c in steps[g, 4]:
            c.start()
    send_slash(4)

    for c in loads[2:]:
        c.wait()
    slash_copies[0].wait_recv()
    key_row = lax.broadcasted_iota(jnp.int32, (TILE, HD), 0)
    key_lane = lax.broadcasted_iota(jnp.int32, (TILE, HD), 1)
    near = slash[0, 1]

    def stacked(i):
        rows = q[pl.ds(pl.multiple_of(i * TILE, TILE), TILE), :]
        return jnp.concatenate([rows[:, h * HD:(h + 1) * HD] for h in range(QPK)], axis=0)

    def soft(scores):
        top = jnp.max(scores, axis=1, keepdims=True)
        return top, jnp.exp2((scores - top) * RATE).astype(BF16)

    def mixed(weights, value_rows):
        ones = jnp.ones(value_rows.shape, BF16)
        return jnp.dot(weights, jnp.concatenate([value_rows, ones], axis=1), preferred_element_type=F32)

    def first(i, _):
        t = ctx * NT + i
        keys = jnp.concatenate([kw[NT + i], kw[i], kw[NT + i - near]], axis=0)
        diagonal = jnp.where((key_row == key_lane) & (key_lane > 0), HIDE, 0.0).astype(BF16)
        far_bias = jnp.where((key_lane == 0) & (key_lane + t < slash[0, 0]), HIDE, 0.0).astype(BF16)
        near_bias = jnp.where((key_lane == 0) & (key_lane + t < near), HIDE, 0.0).astype(BF16)
        bias = jnp.concatenate([diagonal, far_bias, near_bias], axis=0)
        query = jnp.concatenate([stacked(i), causal[...]], axis=1)
        scores = dot_nt(query, jnp.concatenate([keys, bias], axis=1))
        top, weights = soft(scores)
        ebuf_a[i] = weights
        mx[0, i] = jnp.broadcast_to(top, (ROWS, HD))
        return 0

    lax.fori_loop(0, NT, first, 0, unroll=4)

    slash_copies[1].wait_recv()

    def mix(i, _):
        values = jnp.concatenate([vw[NT + i], vw[i], vw[NT + i - near]], axis=0)
        acc0[i] = mixed(ebuf_a[i], values)
        return 0

    lax.fori_loop(0, NT, mix, 0, unroll=4)

    lanes8 = lax.broadcasted_iota(jnp.int32, (8, HD), 1)
    ids = jnp.zeros((8, HD), jnp.int32)
    for j in range(NV):
        ids = jnp.where(lanes8 == j, vert[0, j], ids)
    slot_row = lax.broadcasted_iota(jnp.int32, (G * TILE, HD), 0) // TILE
    slot_lane = lax.broadcasted_iota(jnp.int32, (G * TILE, HD), 1)

    def flags(i):
        t = ctx * NT + i
        valid = (lanes8 < keep[0, i]) & (ids < t) & (ids != t - slash[0, 0]) & (ids != t - near)
        flag = jnp.where(valid | (lanes8 >= NV), 0.0, 1.0)
        return jnp.broadcast_to(flag[:1], (ROWS, HD)).astype(BF16)

    for g in range(NG):
        arrived(g, 4)
        for jj in range(G):
            order = [p if g == 0 else 4 * (p % 4) + p // 4 for p in range(16)]
            kvert[g, jj] = jnp.concatenate([full[g, p, jj] for p in order[:8]], axis=0)
            vvert[g, jj] = jnp.concatenate([full[g, p, jj] for p in order[8:]], axis=0)
        bias = jnp.where(slot_row + g * G == slot_lane, HIDE, 0.0).astype(BF16)

        def vertical(i, _):
            keys = kvert[g].reshape(G * TILE, HD)
            values = vvert[g].reshape(G * TILE, HD)
            query = jnp.concatenate([stacked(i), flags(i)], axis=1)
            scores = dot_nt(query, jnp.concatenate([keys, bias], axis=1))
            top, weights = soft(scores)
            ebuf_b[g, i] = weights
            mx[g + 1, i] = jnp.broadcast_to(top, (ROWS, HD))
            acc[g, i] = mixed(weights, values)
            return 0

        lax.fori_loop(0, NT, vertical, 0, unroll=8)

    lane_id = lax.broadcasted_iota(jnp.int32, (ROWS, HD), 1)
    win_row = lax.broadcasted_iota(jnp.int32, (2 * NT, TILE), 0)
    vs_row = lax.broadcasted_iota(jnp.int32, (NV, TILE), 0)

    def sums(rows, weights, which):
        both = jnp.dot(rows, weights, preferred_element_type=F32)
        return both[which:which + 1] + both[8 + which:9 + which]

    def finish(i, vertical_sums):
        tops = [mx[x, i] for x in range(NG + 1)]
        top = functools.reduce(jnp.maximum, tops)
        scales = [jnp.exp2((t - top) * RATE) for t in tops]
        total = acc0[i, :, HD:] * scales[0]
        for g in range(NG):
            total = total + acc[g, i, :, HD:] * scales[g + 1]
        inverse = 1.0 / total
        scales = [f * inverse for f in scales]
        for x in range(NG + 1):
            sc[x, i] = scales[x]
        factors = scales[0]
        for x in range(1, NG + 1):
            factors = jnp.where(lane_id == x, scales[x], factors)
        turned = jnp.transpose(factors)[:8]
        high = turned.astype(BF16)
        low = (turned - high.astype(F32)).astype(BF16)
        rows = jnp.concatenate([high, low], axis=0)
        shares[i] = rows

        for g in range(NG):
            part = sums(rows, ebuf_b[g, i], g + 1)
            for jj in range(G):
                here = vs_row == g * G + jj
                vertical_sums = vertical_sums + jnp.where(here, part[:, jj * TILE:(jj + 1) * TILE], 0.0)
        return vertical_sums

    vs[...] = lax.fori_loop(0, NT, finish, jnp.zeros((NV, TILE), F32), unroll=8)

    v1[y] = vs[...]
    c1 = [remote(vs, v1.at[y], t_s.at[n], t_r.at[n], p) for n, (_, p) in enumerate(y_peers)]
    for c in c1:
        c.start()

    def near_sums(i, window_sums):
        part = sums(shares[i], ebuf_a[i], 0)
        add = jnp.where(win_row == NT + i, part[:, :TILE], 0.0)
        add = add + jnp.where(win_row == i, part[:, TILE:2 * TILE], 0.0)
        add = add + jnp.where(win_row == NT + i - near, part[:, 2 * TILE:], 0.0)
        return window_sums + add

    win[...] = lax.fori_loop(0, NT, near_sums, jnp.zeros((2 * NT, TILE), F32), unroll=4)
    to_before = remote(win.at[pl.ds(0, NT)], rw, h_s.at[7], h_r.at[7], before)
    to_before.start()
    for c in c1:
        c.wait_recv()
    vz[z] = (v1[0] + v1[1]) + (v1[2] + v1[3])
    c2 = [remote(vz.at[z], vz.at[z], t_s.at[3 + n], t_r.at[3 + n], p) for n, p in enumerate(z_peers)]
    for c in c2:
        c.start()

    def normalise(i, _):
        out = acc0[i, :, :HD] * sc[0, i]
        for g in range(NG):
            out = out + acc[g, i, :, :HD] * sc[g + 1, i]
        out = out.astype(BF16)
        here = pl.ds(pl.multiple_of(i * TILE, TILE), TILE)
        att[here, :] = jnp.concatenate([out[h * TILE:(h + 1) * TILE] for h in range(QPK)], axis=1)
        return 0

    lax.fori_loop(0, NT // 2, normalise, 0)
    to_before.wait_recv()
    hr[head] = win[NT:] + rw[...]
    ch = [remote(hr.at[head], hr.at[head], h_s.at[n], h_r.at[n], p) for n, (_, p) in enumerate(heads)]
    for c in ch:
        c.start()
    lax.fori_loop(NT // 2, NT, normalise, 0)
    for c in ch:
        c.wait_recv()
    total = hr[0]
    for n in range(1, HEADS):
        total = total + hr[n]
    sums_ref[0] = total * (1.0 / (HEADS * QPK))
    for c in [c for group in steps.values() for c in group] + slash_copies + [to_before] + c1:
        c.wait_send()
    for c in c2:
        c.wait_recv()
    total = vz[0]
    for n in range(1, NL * NH):
        total = total + vz[n]
    sums_ref[1] = total * (1.0 / QPK)

    for c in c2 + ch:
        c.wait_send()


def local(queries, keys, values, vertical_ids, slash_offsets, keep_counts):
    rows = keys.shape[0]
    vmem = pl.BlockSpec(memory_space=pltpu.VMEM)
    hbm = pl.BlockSpec(memory_space=pl.ANY)
    dma = pltpu.SemaphoreType.DMA
    attended, both = pl.pallas_call(
        kernel,
        out_shape=(
            pltpu.VMEM(queries.shape, BF16),
            pltpu.VMEM((2, NT, TILE), F32),
        ),
        in_specs=[hbm] * 6,
        out_specs=(vmem, vmem),
        scratch_shapes=[
            *[pltpu.SMEM(a.shape, jnp.int32) for a in (vertical_ids, slash_offsets, keep_counts)],
            pltpu.VMEM((rows, QPK * HD), BF16),
            *[pltpu.VMEM((NT, TILE, HD), BF16) for _ in range(2)],
            *[pltpu.VMEM((2 * NT, TILE, HD), BF16) for _ in range(2)],
            *[pltpu.VMEM((NG, G, TILE, HD), BF16) for _ in range(2)],
            pltpu.VMEM((ROWS, HD), BF16),
            pltpu.VMEM((NT, ROWS, 3 * TILE), BF16),
            pltpu.VMEM((NG, NT, ROWS, G * TILE), BF16),
            pltpu.VMEM((NT, 16, ROWS), BF16),
            pltpu.VMEM((NG + 1, NT, ROWS, HD), F32),
            pltpu.VMEM((NT, ROWS, 2 * HD), F32),
            pltpu.VMEM((NG, NT, ROWS, 2 * HD), F32),
            pltpu.VMEM((NG + 1, NT, ROWS, HD), F32),
            pltpu.VMEM((2 * NT, TILE), F32),
            pltpu.VMEM((NV, TILE), F32),
            pltpu.VMEM((NG, 4, G, 64, HD), BF16),
            *[pltpu.VMEM((NY, G, 64, HD), BF16) for _ in range(2)],
            pltpu.VMEM((NG, NL, G, 16, HD), BF16),
            *[pltpu.VMEM((NL, G, 16, HD), BF16) for _ in range(2)],
            pltpu.VMEM((NG, G, 16, HD), BF16),
            *[pltpu.VMEM((NH, G, 16, HD), BF16) for _ in range(2)],
            pltpu.VMEM((NG, 16, G, 16, HD), BF16),
            pltpu.VMEM((HEADS, NT, TILE), F32),
            pltpu.VMEM((NT, TILE), F32),
            pltpu.VMEM((NY, NV, TILE), F32),
            pltpu.VMEM((NL * NH, NV, TILE), F32),
            dma((8,)), dma((2,)), dma((2,)),
            dma((NG * 15,)), dma((NG * 15,)), dma((4,)), dma((4,)), dma((4,)), dma((4,)), pltpu.SemaphoreType.REGULAR((4,)), dma((18,)), dma((18,)), dma((8,)), dma((8,)),
        ],
        compiler_params=pltpu.CompilerParams(
            collective_id=0, has_side_effects=True, vmem_limit_bytes=56 << 20
        ),
    )(vertical_ids, slash_offsets, keep_counts, queries, keys.reshape(NT, TILE, HD), values.reshape(NT, TILE, HD))
    return attended, both[0].reshape(rows), both[1:]


def solution(mesh):
    placed = (
        P("ctx", "head"),
        P("ctx", "head"),
        P("ctx", "head"),
        P("head", None),
        P("head", None),
        P("head", "ctx"),
    )
    return jax.shard_map(
        local,
        mesh=mesh,
        in_specs=placed,
        out_specs=(P("ctx", "head"), P("ctx"), P("head", None, None)),
        check_vma=False,
    )
```
